512 devices in a mesh: gx: 16 (over y, core), gy: 8 (over x, z_hi), gz: 4 (over z_lo).
Axes of the slice: x: 4, y: 8, z: 8 (z_hi: 2, z_lo: 4; z = z_hi * 4 + z_lo), core: 2. Of those that a mesh axis runs over, the one named last changes fastest.
Arguments:
- upper: float32 [64, 128, 1024], P('gz', 'gx', 'gy'), as said below
- lower: float32 [64, 128, 1024], P('gz', 'gx', 'gy')
- velocity: float32 [3, 64, 128, 1024], P(None, 'gz', 'gx', 'gy'), may hold values from -0.25 to 0.25
- diffusivity: float32 [64, 128, 1024], P('gz', 'gx', 'gy'), may hold values from 0.004 to 0.04
- sensor_center: float32 [4, 16384, 1024], P('gz', ('gx', 'gy')), may hold values from -6 to 6
- sensor_error: float32 [4, 16384], P('gz', ('gx', 'gy')), may hold values from 0.05 to 0.5
- sensor_block: int32 [4, 16384], P('gz', ('gx', 'gy')), may hold values from 0 to 2047, as said below
Outputs:
- upper_out: float32 [64, 128, 1024], P('gz', 'gx', 'gy')
- lower_out: float32 [64, 128, 1024], P('gz', 'gx', 'gy')
The draws below stay inside these ranges and needn't reach their ends.
Inputs may be any that keep to these rules, and one draw needn't show every extreme that they name: `sensor_block`: each entry names a block of the layer of its row (see the steps). In the entries of one device (aligned runs of 128 entries) at most 2 blocks lie on any one device of the layer; in every layer some device holds exactly 2 footprints from every device of the layer. Every entry of upper minus lower is positive.
All inputs are finite; a program needn't handle non-finite values.
Results may differ from the reference program's by a relative error of at most 0.00002.
Values sent between devices are 32-bit elements; how exact they have to be, the bound alone decides.
A program may use at most 64 MiB of HBM per device.

```python
import math
import jax
import jax.numpy as jnp

CX = 8
CY = 128
CZ = 16
S_DEV = 128
CAP = 2
NZ = 64
NX = 128
NY = 1024
SENS_LAYER = 16384
N_GX = 16
N_GY = 8
N_GZ = 4


def bound_parts(key):
    base = jax.random.normal(jax.random.fold_in(key, 21), (NZ, NX, NY), jnp.float32)
    spread = jax.random.uniform(jax.random.fold_in(key, 22), (NZ, NX, NY), jnp.float32, math.log(0.2), math.log(2.0))
    return (base, jnp.exp(spread))


def draw_upper(key, part):
    base, spread = bound_parts(key)
    return base + spread


def draw_lower(key, part):
    base, spread = bound_parts(key)
    return base - spread


def draw_sensor_block(key, part):
    key = jax.random.fold_in(key, 5)
    owners = N_GX * N_GY
    places = owners * CAP
    per_dev = CX // 8 * (CY // 8) * (CZ // 16)
    along_x = CX // 8
    along_y = CY // 8
    wide_y = NY // 8
    wide_x = NX // 8

    def layer(layer_key):
        hottest = jax.random.randint(jax.random.fold_in(layer_key, 1), (), 0, owners)
        weights = jax.random.randint(jax.random.fold_in(layer_key, 2), (owners,), 1, 5)

        def source(source_key):
            owner_of = jnp.arange(places, dtype=jnp.int32) // CAP
            score = jax.random.randint(jax.random.fold_in(source_key, 1), (places,), 0, 4096)
            score = score * weights[owner_of] + (owner_of == hottest).astype(jnp.int32) * 16384
            distinct = score * places + jnp.arange(places, dtype=jnp.int32)
            chosen = jnp.argsort(-distinct, stable=True)[:S_DEV]
            owner = chosen // CAP
            local = jax.random.randint(jax.random.fold_in(source_key, 2), (S_DEV,), 0, per_dev)
            level = local // (along_x * along_y)
            rest = local % (along_x * along_y)
            block_x = owner // N_GY * along_x + rest // along_y
            block_y = owner % N_GY * along_y + rest % along_y
            return level * wide_x * wide_y + block_x * wide_y + block_y
        source_keys = jax.random.split(jax.random.fold_in(layer_key, 3), owners)
        return jax.vmap(source)(source_keys).reshape(-1)
    layer_keys = jax.random.split(key, N_GZ)
    return jax.vmap(layer)(layer_keys).astype(jnp.int32)


def steps_of(rng, shape, cuts, smallest, high):
    level = 1.0
    for position, blocks in cuts:
        steps = jax.random.uniform(jax.random.fold_in(jax.random.fold_in(rng, 6), position), (blocks,), jnp.float32, smallest / len(cuts), high / len(cuts))
        level = level * jnp.repeat(jnp.exp(steps), shape[position] // blocks).reshape((-1,) + (1,) * (len(shape) - 1 - position))
    return level


def scatter_about(stream_key, dims, deviation, bound, shards=(), kind=jnp.bfloat16):
    entries = deviation * jax.random.normal(stream_key, dims, jnp.float32)
    if shards:
        entries = entries * steps_of(stream_key, dims, shards, -0.22, 0.18)
    return jnp.clip(entries, -bound, bound).astype(kind)


def setup_inputs(seed: int = 0) -> dict:
    key_of = jax.random.split(jax.random.key(seed), 8)
    return {
        "upper": draw_upper(jax.random.fold_in(key_of[7], 71), 0),
        "lower": draw_lower(jax.random.fold_in(key_of[7], 71), 0),
        "velocity": jnp.clip(jax.random.uniform(key_of[2], (3, NZ, NX, NY), jnp.float32, -0.25, 0.25) * steps_of(key_of[2], (3, NZ, NX, NY), ((1, 4), (2, 16), (3, 8)), -0.4, 0.0), -0.25, 0.25),
        "diffusivity": jnp.clip(jnp.exp(math.log(0.04) - 2.30258502 * jax.random.uniform(key_of[3], (NZ, NX, NY), jnp.float32) ** steps_of(key_of[3], (NZ, NX, NY), ((0, 4), (1, 16), (2, 8)), -0.2, 0.2)), 0.004, 0.04),
        "sensor_center": scatter_about(key_of[4], (N_GZ, SENS_LAYER, 1024), 1.0, 6.0, ((0, 4), (1, 128)), jnp.float32),
        "sensor_error": jnp.clip(jnp.exp(math.log(0.5) - 2.3025851 * jax.random.uniform(key_of[5], (N_GZ, SENS_LAYER), jnp.float32) ** steps_of(key_of[5], (N_GZ, SENS_LAYER), ((0, 4), (1, 128)), -0.2, 0.2)), 0.05, 0.5),
        "sensor_block": draw_sensor_block(jax.random.fold_in(key_of[7], 71), 0),
    }


def take(field, dim, offset):
    index = [slice(None)]
    for axis in range(1, 4):
        length = field.shape[axis]
        if axis == dim:
            index.append(slice(1 + offset, length - 1 + offset))
        else:
            index.append(slice(1, length - 1))
    return field[tuple(index)]


def advance(padded, coeffs):
    center = take(padded, 1, 0)
    middle = take(coeffs, 1, 0)
    result = center
    nearby = jnp.zeros_like(center)
    for comp in range(3):
        below = take(padded, comp + 1, -1)
        above = take(padded, comp + 1, 1)
        speed_below = take(coeffs, comp + 1, -1)[comp]
        speed_above = take(coeffs, comp + 1, 1)[comp]
        result = result - jnp.abs(middle[comp]) * center + jnp.maximum(speed_below, 0.0) * below + jnp.maximum(-speed_above, 0.0) * above
        nearby = nearby + below + above
    return result + middle[3] * (nearby - 6.0 * center)


def to_blocks(field):
    depth, rows, cols = field.shape
    cut = field.reshape(depth // 16, 16, rows // 8, 8, cols // 8, 8)
    return cut.transpose(0, 2, 4, 1, 3, 5).reshape(-1, 1024)


def from_blocks(blocks, depth, rows, cols):
    cut = blocks.reshape(depth // 16, rows // 8, cols // 8, 16, 8, 8)
    return cut.transpose(0, 3, 1, 4, 2, 5).reshape(depth, rows, cols)


def reference(upper, lower, velocity, diffusivity, sensor_center, sensor_error, sensor_block):
    bounds = jnp.stack([upper, lower])
    coeffs = jnp.concatenate([velocity, diffusivity[None]], axis=0)
    coeffs = jnp.pad(coeffs, ((0, 0), (1, 1), (1, 1), (1, 1)))
    for step in range(2):
        bounds = advance(jnp.pad(bounds, ((0, 0), (1, 1), (1, 1), (1, 1))), coeffs)
    depth, rows, cols = upper.shape
    per_layer = (CZ // 16) * (rows // 8) * (cols // 8)
    layer_ids = jnp.arange(N_GZ, dtype=jnp.int32)[:, None] * per_layer
    target = (layer_ids + sensor_block).reshape(-1).astype(jnp.int32)
    high = (sensor_center + sensor_error[..., None]).reshape(-1, 1024)
    low = (sensor_center - sensor_error[..., None]).reshape(-1, 1024)
    count = per_layer * N_GZ
    ceiling = jnp.full((count, 1024), jnp.inf, dtype=jnp.float32).at[target].min(high)
    floor_table = jnp.full((count, 1024), -jnp.inf, dtype=jnp.float32).at[target].max(low)
    upper_out = from_blocks(jnp.minimum(to_blocks(bounds[0]), ceiling), depth, rows, cols)
    lower_out = from_blocks(jnp.maximum(to_blocks(bounds[1]), floor_table), depth, rows, cols)
    return upper_out, lower_out
```

```python
import jax
import jax.numpy as jnp
from jax import lax
from jax.experimental import pallas as pl
from jax.experimental.pallas import tpu as pltpu
from jax.sharding import PartitionSpec as P

MESH = pl.DeviceIdType.MESH
N_X, N_Y, N_Z = 16, 8, 4
OWNERS = N_X * N_Y
GROUP = 16
GROUPS = OWNERS // GROUP
ROWS = 17
PITCH = 24
UP, LO, VZ, VX, VY, DIFF = range(6)


def peer(i, gx, gy):
    along_y = lax.rem(gx // 2 + lax.rem(i, 8), 8)
    core = lax.rem(lax.rem(gx, 2) + lax.rem(i // 8, 2), 2)
    return along_y * 2 + core, lax.rem(gy + i // 16, N_Y)


def lane_of(shape):
    return lax.broadcasted_iota(jnp.int32, shape, len(shape) - 1)


def merge(tables, block, err, label):
    ceilings, floors = tables
    high = block + err
    low = block - err
    new_c, new_f = [], []
    for b in range(16):
        mine = label == float(b)
        new_c.append(jnp.minimum(ceilings[b], jnp.where(mine, high, jnp.inf)))
        new_f.append(jnp.maximum(floors[b], jnp.where(mine, low, -jnp.inf)))
    return tuple(new_c), tuple(new_f)


def regroup(table):
    rows = list(table)
    group = lane_of((8, 128)) // 8
    for k in (1, 2, 4, 8):
        high = lax.rem(group // k, 2) == 1
        for i in range(16):
            if i & k == 0:
                a, b = rows[i], rows[i | k]
                rows[i] = jnp.where(high, pltpu.roll(b, 8 * k, 1), a)
                rows[i | k] = jnp.where(high, b, pltpu.roll(a, 128 - 8 * k, 1))
    return rows


def kernel(
    upper, lower, velocity, diffusivity, center, error, block,
    upper_out, lower_out,
    fields, coefs, stage, err_v, blk_v, msg, got, ceil_t, floor_t, flat,
    zs, zr, xs, xr, ys, yr, turn,
    in_sem, c_sem, send_sem, recv_sem, face_send, face_recv,
):
    gx, gy, gz = lax.axis_index("gx"), lax.axis_index("gy"), lax.axis_index("gz")

    barrier = pltpu.get_barrier_semaphore()

    def greet(i, carry):
        px, py = peer(i, gx, gy)
        pl.semaphore_signal(barrier, inc=1, device_id=(px, py, gz), device_id_type=MESH)
        return carry

    lax.fori_loop(1, OWNERS, greet, 0)
    for d in (1, N_Z - 1):
        pl.semaphore_signal(
            barrier, inc=1, device_id=(gx, gy, lax.rem(gz + d, N_Z)), device_id_type=MESH
        )

    loads = [
        pltpu.make_async_copy(error, err_v, c_sem.at[0]),
        pltpu.make_async_copy(block, blk_v, c_sem.at[1]),
        pltpu.make_async_copy(center.at[0], stage, c_sem.at[2]),
    ]
    field_loads = [
        pltpu.make_async_copy(upper, fields.at[UP], in_sem.at[0]),
        pltpu.make_async_copy(lower, fields.at[LO], in_sem.at[1]),
        pltpu.make_async_copy(velocity, fields.at[pl.ds(VZ, 3)], in_sem.at[2]),
        pltpu.make_async_copy(diffusivity, fields.at[DIFF], in_sem.at[3]),
    ]
    for c in loads + field_loads:
        c.start()

    loads[0].wait()
    loads[1].wait()
    blk = blk_v[...]
    block_y = jnp.bitwise_and(blk, 127)
    owner = (blk // 128) * N_Y + block_y // 16
    local = jnp.bitwise_and(block_y, 15).astype(jnp.float32)
    dest = lax.broadcasted_iota(jnp.int32, (OWNERS, 128), 0)
    sensor = lane_of((OWNERS, 128))
    goes = jnp.broadcast_to(owner, (OWNERS, 128)) == dest
    before = jnp.where(dest < sensor, 1.0, 0.0).astype(jnp.bfloat16)
    rank = jnp.dot(
        jnp.where(goes, 1.0, 0.0).astype(jnp.bfloat16), before, preferred_element_type=jnp.float32
    )
    picks = [jnp.logical_and(goes, rank < 0.5), jnp.logical_and(goes, rank > 0.5)]
    meta = jnp.full((OWNERS, 128), -1.0, jnp.float32)
    for r in range(2):
        e = jnp.sum(jnp.where(picks[r], err_v[...], 0.0), axis=1, keepdims=True)
        l = jnp.sum(jnp.where(picks[r], local + 1.0, 0.0), axis=1, keepdims=True) - 1.0
        meta = jnp.where(sensor == 2 * r, e, meta)
        meta = jnp.where(sensor == 2 * r + 1, l, meta)
    msg[pl.ds(16, OWNERS, stride=PITCH), :] = meta
    pick = jnp.concatenate([jnp.where(p, 1.0, 0.0) for p in picks], axis=0).astype(jnp.bfloat16)
    loads[2].wait()
    for j in range(8):
        whole = stage[:, j * 128 : (j + 1) * 128]
        part_a = whole.astype(jnp.bfloat16)
        rest = whole - part_a.astype(jnp.float32)
        part_b = rest.astype(jnp.bfloat16)
        part_c = (rest - part_b.astype(jnp.float32)).astype(jnp.bfloat16)
        out = jnp.dot(pick, part_a, preferred_element_type=jnp.float32)
        out += jnp.dot(pick, part_b, preferred_element_type=jnp.float32)
        out += jnp.dot(pick, part_c, preferred_element_type=jnp.float32)
        msg[pl.ds(j, OWNERS, stride=PITCH), :] = out[:OWNERS]
        msg[pl.ds(8 + j, OWNERS, stride=PITCH), :] = out[OWNERS:]

    for c in field_loads:
        c.wait()

    def fill_faces(values, speeds):
        for k, v in enumerate(values):
            zs[0, 8 * k : 8 * k + 8, :] = v[15]
            zs[1, 8 * k : 8 * k + 8, :] = v[0]
            xs[0, 16 * k : 16 * k + 16, :] = v[:, 7, :]
            xs[1, 16 * k : 16 * k + 16, :] = v[:, 0, :]
            t = v.reshape(128, 128).T
            ys[0, k : k + 1, :] = t[127:128]
            ys[1, k : k + 1, :] = t[0:1]
        if speeds is not None:
            vz, vx, vy = speeds
            zs[0, 16:24, :] = vz[15]
            zs[1, 16:24, :] = vz[0]
            xs[0, 32:48, :] = vx[:, 7, :]
            xs[1, 32:48, :] = vx[:, 0, :]
            t = vy.reshape(128, 128).T
            ys[0, 2:3, :] = t[127:128]
            ys[1, 2:3, :] = t[0:1]

    def face_copies(rnd):
        copies = []
        for d in range(2):
            step = 1 if d == 0 else -1
            for k, (src, dst, dev) in enumerate((
                (zs, zr, (gx, gy, lax.rem(gz + step + N_Z, N_Z))),
                (xs, xr, (lax.rem(gx + step + N_X, N_X), gy, gz)),
                (ys, yr, (gx, lax.rem(gy + step + N_Y, N_Y), gz)),
            )):
                n = src.shape[1]
                if rnd == 1 and k < 2:
                    n = n // 3 * 2
                copies.append(
                    pltpu.make_async_remote_copy(
                        src_ref=src.at[d, pl.ds(0, n)],
                        dst_ref=dst.at[rnd, d, pl.ds(0, n)],
                        send_sem=face_send.at[rnd, d, k],
                        recv_sem=face_recv.at[rnd, d, k],
                        device_id=dev,
                        device_id_type=MESH,
                    )
                )
        return copies

    fill_faces([fields[UP], fields[LO]], [fields[VZ], fields[VX], fields[VY]])

    pl.semaphore_wait(barrier, OWNERS - 1 + 2)

    first = face_copies(0)
    for c in first:
        c.start()

    def message(i):
        px, py = peer(i, gx, gy)
        at = pl.multiple_of((px * N_Y + py) * PITCH, 8)
        return pltpu.make_async_remote_copy(
            src_ref=msg.at[pl.ds(at, ROWS)],
            dst_ref=got.at[i, pl.ds(0, ROWS)],
            send_sem=send_sem,
            recv_sem=recv_sem.at[i // GROUP],
            device_id=(px, py, gz),
            device_id_type=MESH,
        )

    def send(i, carry):
        message(i).start()
        return carry

    lax.fori_loop(1, OWNERS, send, 0)

    x_of = lax.broadcasted_iota(jnp.int32, (16, 8, 128), 1)
    y_of = lax.broadcasted_iota(jnp.int32, (16, 8, 128), 2)
    inner = [
        (gz > 0, gz < N_Z - 1),
        (gx > 0, gx < N_X - 1),
        (gy > 0, gy < N_Y - 1),
    ]

    def keep(flag, value):
        return jnp.where(flag, value, 0.0)

    def halo(rnd, dim, k, side):
        flag = inner[dim][side]
        if dim == 0:
            return keep(flag, zr[rnd, side, 8 * k : 8 * k + 8, :])[None]
        if dim == 1:
            return keep(flag, xr[rnd, side, 16 * k : 16 * k + 16, :])[:, None, :]
        columns = turned[side][:, k : k + 1]
        return keep(flag, columns).reshape(16, 8, 1)

    def shifted(value, rnd, dim, k):
        below, above = halo(rnd, dim, k, 0), halo(rnd, dim, k, 1)
        if dim == 0:
            return (
                jnp.concatenate([below, value[:15]], axis=0),
                jnp.concatenate([value[1:], above], axis=0),
            )
        if dim == 1:
            return (
                jnp.where(x_of == 0, below, pltpu.roll(value, 1, 1)),
                jnp.where(x_of == 7, above, pltpu.roll(value, 7, 1)),
            )
        return (
            jnp.where(y_of == 0, below, pltpu.roll(value, 1, 2)),
            jnp.where(y_of == 127, above, pltpu.roll(value, 127, 2)),
        )

    turn[...] = jnp.zeros_like(turn)

    def turn_faces(rnd):
        sides = []
        for d in range(2):
            turn[d, 0:8, :] = yr[rnd, d]
            sides.append(turn[d].T)
        return sides

    for c in first:
        c.wait()
    turned = turn_faces(0)
    diff = fields[DIFF]
    centre = 1.0 - 6.0 * diff
    for dim, which in enumerate((VZ, VX, VY)):
        v = fields[which]
        centre = centre - jnp.abs(v)
        v_below, v_above = shifted(v, 0, dim, 2)
        coefs[2 * dim] = jnp.maximum(v_below, 0.0) + diff
        coefs[2 * dim + 1] = jnp.maximum(-v_above, 0.0) + diff
    coefs[6] = centre

    def advance(rnd):
        results = []
        for k in range(2):
            value = fields[k]
            total = coefs[6] * value
            for dim in range(3):
                below, above = shifted(value, rnd, dim, k)
                total = total + coefs[2 * dim] * below + coefs[2 * dim + 1] * above
            results.append(total)
        return results

    once = advance(0)
    fields[UP] = once[0]
    fields[LO] = once[1]
    fill_faces([fields[UP], fields[LO]], None)
    second = face_copies(1)
    for c in second:
        c.start()

    def tables():
        return (
            tuple(ceil_t[b] for b in range(16)),
            tuple(floor_t[b] for b in range(16)),
        )

    def store(t):
        for b in range(16):
            ceil_t[b] = t[0][b]
            floor_t[b] = t[1][b]

    def take(t, rows, meta):
        for r in range(2):
            err = jnp.broadcast_to(meta[:, 2 * r : 2 * r + 1], (8, 128))
            label = jnp.broadcast_to(meta[:, 2 * r + 1 : 2 * r + 2], (8, 128))
            t = merge(t, rows(r), err, label)
        return t

    full = lambda v: jnp.full((8, 128), v, jnp.float32)
    own = (gx * N_Y + gy) * PITCH
    start = (tuple(full(jnp.inf) for _ in range(16)), tuple(full(-jnp.inf) for _ in range(16)))
    store(
        take(
            start,
            lambda r: msg[pl.ds(pl.multiple_of(own + 8 * r, 8), 8), :],
            msg[pl.ds(pl.multiple_of(own + 16, 8), 8), :][0:1],
        )
    )

    def await_group(g):
        lo = max(g * GROUP, 1)
        n = (g + 1) * GROUP - lo
        for_all = pltpu.make_async_remote_copy(
            src_ref=got.at[pl.ds(lo, n), pl.ds(0, ROWS)],
            dst_ref=got.at[pl.ds(lo, n), pl.ds(0, ROWS)],
            send_sem=send_sem,
            recv_sem=recv_sem.at[g],
            device_id=(gx, gy, gz),
            device_id_type=MESH,
        )
        for_all.wait_recv()

        def body(i, t):
            return take(t, lambda r: got[i, 8 * r : 8 * r + 8, :], got[i, 16:24, :][0:1])

        store(lax.fori_loop(lo, lo + n, body, tables()))

    await_group(0)

    for c in second:
        c.wait()
    turned = turn_faces(1)
    twice = advance(1)
    fields[UP] = twice[0]
    fields[LO] = twice[1]

    for g in range(1, GROUPS):
        await_group(g)

    for table, which, out in ((ceil_t, UP, upper_out), (floor_t, LO, lower_out)):
        rows = regroup([table[b] for b in range(16)])
        for g in range(16):
            flat[pl.ds(g, 8, stride=16), :] = rows[g]
        pick_of = jnp.minimum if which == UP else jnp.maximum
        out[...] = pick_of(fields[which], flat[...].reshape(16, 8, 128))

    def sent(i, carry):
        message(i).wait_send()
        return carry

    lax.fori_loop(1, OWNERS, sent, 0)


def shards(*args):
    f32 = jnp.float32
    dma = pltpu.SemaphoreType.DMA
    return pl.pallas_call(
        kernel,
        out_shape=[jax.ShapeDtypeStruct((16, 8, 128), f32)] * 2,
        in_specs=[pl.BlockSpec(memory_space=pl.ANY)] * 7,
        out_specs=[pl.BlockSpec(memory_space=pltpu.VMEM)] * 2,
        scratch_shapes=[
            pltpu.VMEM((6, 16, 8, 128), f32),
            pltpu.VMEM((7, 16, 8, 128), f32),
            pltpu.VMEM((128, 1024), f32),
            pltpu.VMEM((1, 128), f32),
            pltpu.VMEM((1, 128), jnp.int32),
            pltpu.VMEM((OWNERS * PITCH, 128), f32),
            pltpu.VMEM((OWNERS, PITCH, 128), f32),
            pltpu.VMEM((16, 8, 128), f32),
            pltpu.VMEM((16, 8, 128), f32),
            pltpu.VMEM((128, 128), f32),
            pltpu.VMEM((2, 24, 128), f32),
            pltpu.VMEM((2, 2, 24, 128), f32),
            pltpu.VMEM((2, 48, 128), f32),
            pltpu.VMEM((2, 2, 48, 128), f32),
            pltpu.VMEM((2, 8, 128), f32),
            pltpu.VMEM((2, 2, 8, 128), f32),
            pltpu.VMEM((2, 128, 128), f32),
            dma((4,)),
            dma((3,)),
            dma,
            dma((GROUPS,)),
            dma((2, 2, 3)),
            dma((2, 2, 3)),
        ],
        compiler_params=pltpu.CompilerParams(
            collective_id=0, has_side_effects=True, vmem_limit_bytes=32 << 20
        ),
        cost_estimate=pl.CostEstimate(flops=10**8, bytes_accessed=2 << 20, transcendentals=0),
    )(*args)


def solution(mesh):
    in_specs = (
        P("gz", "gx", "gy"),
        P("gz", "gx", "gy"),
        P(None, "gz", "gx", "gy"),
        P("gz", "gx", "gy"),
        P("gz", ("gx", "gy"), None),
        P("gz", ("gx", "gy")),
        P("gz", ("gx", "gy")),
    )
    out_specs = (P("gz", "gx", "gy"), P("gz", "gx", "gy"))
    return jax.shard_map(shards, mesh=mesh, in_specs=in_specs, out_specs=out_specs, check_vma=False)
```

```python
import jax
import jax.numpy as jnp
from jax import lax
from jax.experimental import pallas as pl
from jax.experimental.pallas import tpu as pltpu
from jax.sharding import PartitionSpec as P

MESH = pl.DeviceIdType.MESH
N_X, N_Y, N_Z = 16, 8, 4
OWNERS = N_X * N_Y
GROUP = 16
GROUPS = OWNERS // GROUP
ROWS = 17
PITCH = 24
UP, LO, VZ, VX, VY, DIFF = range(6)


def peer(i, gx, gy):
    along_x = ((gx >> 1) + i) & 7
    core = (gx ^ (i >> 3)) & 1
    return along_x * 2 + core, (gy + (i >> 4)) & (N_Y - 1)


def lane_of(shape):
    return lax.broadcasted_iota(jnp.int32, shape, len(shape) - 1)


def merge(tables, block, err, label):
    ceilings, floors = tables
    high = block + err
    low = block - err
    new_c, new_f = [], []
    for b in range(16):
        mine = label == float(b)
        new_c.append(jnp.minimum(ceilings[b], jnp.where(mine, high, jnp.inf)))
        new_f.append(jnp.maximum(floors[b], jnp.where(mine, low, -jnp.inf)))
    return tuple(new_c), tuple(new_f)


def regroup(table):
    rows = list(table)
    group = lane_of((8, 128)) // 8
    for k in (1, 2, 4, 8):
        high = lax.rem(group // k, 2) == 1
        for i in range(16):
            if i & k == 0:
                a, b = rows[i], rows[i | k]
                rows[i] = jnp.where(high, pltpu.roll(b, 8 * k, 1), a)
                rows[i | k] = jnp.where(high, b, pltpu.roll(a, 128 - 8 * k, 1))
    return rows


def kernel(
    upper, lower, velocity, diffusivity, center, error, block,
    upper_out, lower_out,
    fields, coefs, stage, err_v, blk_v, msg, got, ceil_t, floor_t, flat,
    zs, zr, xs, xr, ys, yr, turn, wide,
    in_sem, c_sem, send_sem, recv_sem, face_send, face_recv,
):
    gx, gy, gz = lax.axis_index("gx"), lax.axis_index("gy"), lax.axis_index("gz")

    loads = [
        pltpu.make_async_copy(error, err_v, c_sem.at[0]),
        pltpu.make_async_copy(block, blk_v, c_sem.at[1]),
        pltpu.make_async_copy(center.at[0], stage, c_sem.at[2]),
    ]
    field_loads = [
        pltpu.make_async_copy(upper, fields.at[UP], in_sem.at[0]),
        pltpu.make_async_copy(lower, fields.at[LO], in_sem.at[1]),
        pltpu.make_async_copy(velocity, fields.at[pl.ds(VZ, 3)], in_sem.at[2]),
        pltpu.make_async_copy(diffusivity, fields.at[DIFF], in_sem.at[3]),
    ]
    for c in loads + field_loads:
        c.start()

    barrier = pltpu.get_barrier_semaphore()

    def greet(i, carry):
        px, py = peer(i, gx, gy)
        pl.semaphore_signal(barrier, inc=1, device_id=(px, py, gz), device_id_type=MESH)
        return carry

    lax.fori_loop(1, OWNERS, greet, 0)
    for d in (1, N_Z - 1):
        pl.semaphore_signal(
            barrier, inc=1, device_id=(gx, gy, lax.rem(gz + d, N_Z)), device_id_type=MESH
        )

    loads[0].wait()
    loads[1].wait()
    blk = blk_v[...]
    block_y = jnp.bitwise_and(blk, 127)
    owner = (blk // 128) * N_Y + block_y // 16
    local = jnp.bitwise_and(block_y, 15).astype(jnp.float32)
    dest = lax.broadcasted_iota(jnp.int32, (OWNERS, 128), 0)
    sensor = lane_of((OWNERS, 128))
    goes = jnp.broadcast_to(owner, (OWNERS, 128)) == dest
    before = jnp.where(dest < sensor, 1.0, 0.0).astype(jnp.bfloat16)
    rank = jnp.dot(
        jnp.where(goes, 1.0, 0.0).astype(jnp.bfloat16), before, preferred_element_type=jnp.float32
    )
    picks = [jnp.logical_and(goes, rank < 0.5), jnp.logical_and(goes, rank > 0.5)]
    meta = jnp.full((OWNERS, 128), -1.0, jnp.float32)
    for r in range(2):
        e = jnp.sum(jnp.where(picks[r], err_v[...], 0.0), axis=1, keepdims=True)
        l = jnp.sum(jnp.where(picks[r], local + 1.0, 0.0), axis=1, keepdims=True) - 1.0
        meta = jnp.where(sensor == 2 * r, e, meta)
        meta = jnp.where(sensor == 2 * r + 1, l, meta)
    msg[pl.ds(16, OWNERS, stride=PITCH), :] = meta
    pick = jnp.concatenate([jnp.where(p, 1.0, 0.0) for p in picks], axis=0).astype(jnp.bfloat16)
    loads[2].wait()
    for j in range(8):
        whole = stage[:, j * 128 : (j + 1) * 128]
        part_a = whole.astype(jnp.bfloat16)
        rest = whole - part_a.astype(jnp.float32)
        part_b = rest.astype(jnp.bfloat16)
        part_c = (rest - part_b.astype(jnp.float32)).astype(jnp.bfloat16)
        out = jnp.dot(pick, part_a, preferred_element_type=jnp.float32)
        out += jnp.dot(pick, part_b, preferred_element_type=jnp.float32)
        out += jnp.dot(pick, part_c, preferred_element_type=jnp.float32)
        msg[pl.ds(j, OWNERS, stride=PITCH), :] = out[:OWNERS]
        msg[pl.ds(8 + j, OWNERS, stride=PITCH), :] = out[OWNERS:]

    for c in field_loads:
        c.wait()

    def fill_faces(values, speeds):
        for k, v in enumerate(values):
            zs[0, 8 * k : 8 * k + 8, :] = v[15]
            zs[1, 8 * k : 8 * k + 8, :] = v[0]
            xs[0, 16 * k : 16 * k + 16, :] = v[:, 7, :]
            xs[1, 16 * k : 16 * k + 16, :] = v[:, 0, :]
            t = v.reshape(128, 128).T
            ys[0, k : k + 1, :] = t[127:128]
            ys[1, k : k + 1, :] = t[0:1]
        if speeds is not None:
            vz, vx, vy = speeds
            zs[0, 16:24, :] = vz[15]
            zs[1, 16:24, :] = vz[0]
            xs[0, 32:48, :] = vx[:, 7, :]
            xs[1, 32:48, :] = vx[:, 0, :]
            t = vy.reshape(128, 128).T
            ys[0, 2:3, :] = t[127:128]
            ys[1, 2:3, :] = t[0:1]

    def face_copies(rnd):
        copies = []
        for d in range(2):
            step = 1 if d == 0 else -1
            for k, (src, dst, dev) in enumerate((
                (zs, zr, (gx, gy, lax.rem(gz + step + N_Z, N_Z))),
                (xs, xr, (lax.rem(gx + step + N_X, N_X), gy, gz)),
                (ys, yr, (gx, lax.rem(gy + step + N_Y, N_Y), gz)),
            )):
                n = src.shape[1]
                if rnd == 1 and k < 2:
                    n = n // 3 * 2
                copies.append(
                    pltpu.make_async_remote_copy(
                        src_ref=src.at[d, pl.ds(0, n)],
                        dst_ref=dst.at[rnd, d, pl.ds(0, n)],
                        send_sem=face_send.at[rnd, d, k],
                        recv_sem=face_recv.at[rnd, d, k],
                        device_id=dev,
                        device_id_type=MESH,
                    )
                )
        return copies

    fill_faces([fields[UP], fields[LO]], [fields[VZ], fields[VX], fields[VY]])

    pl.semaphore_wait(barrier, OWNERS - 1 + 2)

    first = face_copies(0)
    for c in first:
        c.start()

    def message(i):
        px, py = peer(i, gx, gy)
        at = pl.multiple_of((px * N_Y + py) * PITCH, 8)
        return pltpu.make_async_remote_copy(
            src_ref=msg.at[pl.ds(at, ROWS)],
            dst_ref=got.at[i, pl.ds(0, ROWS)],
            send_sem=send_sem,
            recv_sem=recv_sem.at[i >> 4],
            device_id=(px, py, gz),
            device_id_type=MESH,
        )

    def send(i, carry):
        message(i).start()
        return carry

    lax.fori_loop(1, OWNERS, send, 0)

    x_of = lax.broadcasted_iota(jnp.int32, (16, 8, 128), 1)
    y_of = lax.broadcasted_iota(jnp.int32, (16, 8, 128), 2)
    inner = [
        (gz > 0, gz < N_Z - 1),
        (gx > 0, gx < N_X - 1),
        (gy > 0, gy < N_Y - 1),
    ]

    def keep(flag, value):
        return jnp.where(flag, value, 0.0)

    def halo(rnd, dim, k, side):
        flag = inner[dim][side]
        if dim == 0:
            return keep(flag, zr[rnd, side, 8 * k : 8 * k + 8, :])[None]
        if dim == 1:
            return keep(flag, xr[rnd, side, 16 * k : 16 * k + 16, :])[:, None, :]
        columns = turned[side][:, k : k + 1]
        return keep(flag, columns).reshape(16, 8, 1)

    def shifted(value, rnd, dim, k):
        below, above = halo(rnd, dim, k, 0), halo(rnd, dim, k, 1)
        if dim == 0:
            return (
                jnp.concatenate([below, value[:15]], axis=0),
                jnp.concatenate([value[1:], above], axis=0),
            )
        if dim == 1:
            return (
                jnp.where(x_of == 0, below, pltpu.roll(value, 1, 1)),
                jnp.where(x_of == 7, above, pltpu.roll(value, 7, 1)),
            )
        return (
            jnp.where(y_of == 0, below, pltpu.roll(value, 1, 2)),
            jnp.where(y_of == 127, above, pltpu.roll(value, 127, 2)),
        )

    turn[...] = jnp.zeros_like(turn)

    def turn_faces(rnd):
        sides = []
        for d in range(2):
            turn[d, 0:8, :] = yr[rnd, d]
            sides.append(turn[d].T)
        return sides

    for c in first:
        c.wait()
    turned = turn_faces(0)
    diff = fields[DIFF]
    centre = 1.0 - 6.0 * diff
    for dim, which in enumerate((VZ, VX, VY)):
        v = fields[which]
        centre = centre - jnp.abs(v)
        v_below, v_above = shifted(v, 0, dim, 2)
        coefs[2 * dim] = jnp.maximum(v_below, 0.0) + diff
        coefs[2 * dim + 1] = jnp.maximum(-v_above, 0.0) + diff
    coefs[6] = centre

    def advance(rnd):
        results = []
        for k in range(2):
            value = fields[k]
            total = coefs[6] * value
            for dim in range(3):
                below, above = shifted(value, rnd, dim, k)
                total = total + coefs[2 * dim] * below + coefs[2 * dim + 1] * above
            results.append(total)
        return results

    once = advance(0)
    fields[UP] = once[0]
    fields[LO] = once[1]
    fill_faces([fields[UP], fields[LO]], None)
    second = face_copies(1)
    for c in second:
        c.start()

    def tables():
        return (
            tuple(ceil_t[b] for b in range(16)),
            tuple(floor_t[b] for b in range(16)),
        )

    def store(t):
        for b in range(16):
            ceil_t[b] = t[0][b]
            floor_t[b] = t[1][b]

    def spread(m, row):
        for k in range(4):
            wide[4 * m + k] = jnp.broadcast_to(row[:, k : k + 1], (8, 128))

    def take(t, m, rows):
        for r in range(2):
            t = merge(t, rows(r), wide[4 * m + 2 * r], wide[4 * m + 2 * r + 1])
        return t

    full = lambda v: jnp.full((8, 128), v, jnp.float32)
    own = (gx * N_Y + gy) * PITCH
    start = (tuple(full(jnp.inf) for _ in range(16)), tuple(full(-jnp.inf) for _ in range(16)))
    spread(0, msg[pl.ds(pl.multiple_of(own + 16, 8), 8), :][0:1])
    store(take(start, 0, lambda r: msg[pl.ds(pl.multiple_of(own + 8 * r, 8), 8), :]))

    def await_group(g):
        lo = max(g * GROUP, 1)
        n = (g + 1) * GROUP - lo
        for_all = pltpu.make_async_remote_copy(
            src_ref=got.at[pl.ds(lo, n), pl.ds(0, ROWS)],
            dst_ref=got.at[pl.ds(lo, n), pl.ds(0, ROWS)],
            send_sem=send_sem,
            recv_sem=recv_sem.at[g],
            device_id=(gx, gy, gz),
            device_id_type=MESH,
        )
        for_all.wait_recv()
        for m in range(n):
            spread(m, got[lo + m, 16:17, :])

        def one(m, t):
            return take(t, m, lambda r: got[lo + m, 8 * r : 8 * r + 8, :])

        def body(h, t):
            return one(2 * h + 1, one(2 * h, t))

        t = lax.fori_loop(0, n // 2, body, tables())
        store(one(n - 1, t) if n % 2 else t)

    await_group(0)

    for c in second:
        c.wait()
    turned = turn_faces(1)
    twice = advance(1)
    fields[UP] = twice[0]
    fields[LO] = twice[1]

    for g in range(1, GROUPS):
        await_group(g)

    for table, which, out in ((ceil_t, UP, upper_out), (floor_t, LO, lower_out)):
        rows = regroup([table[b] for b in range(16)])
        for g in range(16):
            flat[pl.ds(g, 8, stride=16), :] = rows[g]
        pick_of = jnp.minimum if which == UP else jnp.maximum
        out[...] = pick_of(fields[which], flat[...].reshape(16, 8, 128))

    def sent(i, carry):
        message(i).wait_send()
        return carry

    lax.fori_loop(1, OWNERS, sent, 0)


def shards(*args):
    f32 = jnp.float32
    dma = pltpu.SemaphoreType.DMA
    return pl.pallas_call(
        kernel,
        out_shape=[jax.ShapeDtypeStruct((16, 8, 128), f32)] * 2,
        in_specs=[pl.BlockSpec(memory_space=pl.ANY)] * 7,
        out_specs=[pl.BlockSpec(memory_space=pltpu.VMEM)] * 2,
        scratch_shapes=[
            pltpu.VMEM((6, 16, 8, 128), f32),
            pltpu.VMEM((7, 16, 8, 128), f32),
            pltpu.VMEM((128, 1024), f32),
            pltpu.VMEM((1, 128), f32),
            pltpu.VMEM((1, 128), jnp.int32),
            pltpu.VMEM((OWNERS * PITCH, 128), f32),
            pltpu.VMEM((OWNERS, PITCH, 128), f32),
            pltpu.VMEM((16, 8, 128), f32),
            pltpu.VMEM((16, 8, 128), f32),
            pltpu.VMEM((128, 128), f32),
            pltpu.VMEM((2, 24, 128), f32),
            pltpu.VMEM((2, 2, 24, 128), f32),
            pltpu.VMEM((2, 48, 128), f32),
            pltpu.VMEM((2, 2, 48, 128), f32),
            pltpu.VMEM((2, 8, 128), f32),
            pltpu.VMEM((2, 2, 8, 128), f32),
            pltpu.VMEM((2, 128, 128), f32),
            pltpu.VMEM((4 * GROUP, 8, 128), f32),
            dma((4,)),
            dma((3,)),
            dma,
            dma((GROUPS,)),
            dma((2, 2, 3)),
            dma((2, 2, 3)),
        ],
        compiler_params=pltpu.CompilerParams(
            collective_id=0, has_side_effects=True, vmem_limit_bytes=56 << 20
        ),
        cost_estimate=pl.CostEstimate(flops=10**8, bytes_accessed=2 << 20, transcendentals=0),
    )(*args)


def solution(mesh):
    in_specs = (
        P("gz", "gx", "gy"),
        P("gz", "gx", "gy"),
        P(None, "gz", "gx", "gy"),
        P("gz", "gx", "gy"),
        P("gz", ("gx", "gy"), None),
        P("gz", ("gx", "gy")),
        P("gz", ("gx", "gy")),
    )
    out_specs = (P("gz", "gx", "gy"), P("gz", "gx", "gy"))
    return jax.shard_map(shards, mesh=mesh, in_specs=in_specs, out_specs=out_specs, check_vma=False)
```

```python
import jax
import jax.numpy as jnp
from jax import lax
from jax.experimental import pallas as pl
from jax.experimental.pallas import tpu as pltpu
from jax.sharding import PartitionSpec as P

MESH = pl.DeviceIdType.MESH
N_X, N_Y, N_Z = 16, 8, 4
OWNERS = N_X * N_Y
HALF = OWNERS // 2
FAR = ((1, 16), (16, 32), (32, 48), (48, 64))
NEAR = ((1, 16), (16, 32), (32, 48), (48, 60), (60, 64))
ROWS = (17, 16)
PITCH = 24
UP, LO, VZ, VX, VY, DIFF = range(6)


def peer(i, gx, gy):
    along_y = ((gx >> 1) + i) & 7
    core = (gx ^ (i >> 3)) & 1
    return along_y * 2 + core, (gy + 2 * (i >> 4)) & (N_Y - 1)


def lane_of(shape):
    return lax.broadcasted_iota(jnp.int32, shape, len(shape) - 1)


def merge(tables, block, err, label):
    ceilings, floors = tables
    high = block + err
    low = block - err
    new_c, new_f = [], []
    for b in range(16):
        mine = label == float(b)
        new_c.append(jnp.minimum(ceilings[b], jnp.where(mine, high, jnp.inf)))
        new_f.append(jnp.maximum(floors[b], jnp.where(mine, low, -jnp.inf)))
    return tuple(new_c), tuple(new_f)


def regroup(table):
    rows = list(table)
    group = lane_of((8, 128)) // 8
    for k in (1, 2, 4, 8):
        high = lax.rem(group // k, 2) == 1
        for i in range(16):
            if i & k == 0:
                a, b = rows[i], rows[i | k]
                rows[i] = jnp.where(high, pltpu.roll(b, 8 * k, 1), a)
                rows[i | k] = jnp.where(high, b, pltpu.roll(a, 128 - 8 * k, 1))
    return rows


def kernel(
    upper, lower, velocity, diffusivity, center, error, block,
    upper_out, lower_out,
    fields, coefs, stage, err_v, blk_v, msg, got, ceil_t, floor_t, flat,
    zs, zr, xs, xr, ys, yr, turn, wide, relay, relayed,
    in_sem, c_sem, send_sem, far_sem, near_sem, relay_sem, face_send, face_recv,
):
    gx, gy, gz = lax.axis_index("gx"), lax.axis_index("gy"), lax.axis_index("gz")

    loads = [
        pltpu.make_async_copy(error, err_v, c_sem.at[0]),
        pltpu.make_async_copy(block, blk_v, c_sem.at[1]),
        pltpu.make_async_copy(center.at[0], stage, c_sem.at[2]),
    ]
    field_loads = [
        pltpu.make_async_copy(upper, fields.at[UP], in_sem.at[0]),
        pltpu.make_async_copy(lower, fields.at[LO], in_sem.at[1]),
        pltpu.make_async_copy(velocity, fields.at[pl.ds(VZ, 3)], in_sem.at[2]),
        pltpu.make_async_copy(diffusivity, fields.at[DIFF], in_sem.at[3]),
    ]
    for c in loads + field_loads:
        c.start()

    barrier = pltpu.get_barrier_semaphore()

    def greet(i, carry):
        px, py = peer(i, gx, gy)
        pl.semaphore_signal(barrier, inc=1, device_id=(px, py, gz), device_id_type=MESH)
        return carry

    mirror = (gx, gy ^ 1, gz)
    sideways = (gx, (gy + jnp.where((gy & 1) == 0, N_Y - 1, 1)) & (N_Y - 1), gz)
    others = [mirror, sideways] + [(gx, gy, (gz + d) & (N_Z - 1)) for d in (1, N_Z - 1)]
    for dev in others:
        pl.semaphore_signal(barrier, inc=1, device_id=dev, device_id_type=MESH)
    lax.fori_loop(1, HALF, greet, 0)

    loads[0].wait()
    loads[1].wait()
    blk = blk_v[...]
    block_y = jnp.bitwise_and(blk, 127)
    owner = (blk // 128) * N_Y + block_y // 16
    local = jnp.bitwise_and(block_y, 15).astype(jnp.float32)
    dest = lax.broadcasted_iota(jnp.int32, (OWNERS, 128), 0)
    sensor = lane_of((OWNERS, 128))
    goes = jnp.broadcast_to(owner, (OWNERS, 128)) == dest
    before = jnp.where(dest < sensor, 1.0, 0.0).astype(jnp.bfloat16)
    rank = jnp.dot(
        jnp.where(goes, 1.0, 0.0).astype(jnp.bfloat16), before, preferred_element_type=jnp.float32
    )
    picks = [jnp.logical_and(goes, rank < 0.5), jnp.logical_and(goes, rank > 0.5)]
    meta = jnp.full((OWNERS, 128), -1.0, jnp.float32)
    for r in range(2):
        e = jnp.sum(jnp.where(picks[r], err_v[...], 0.0), axis=1, keepdims=True)
        l = jnp.sum(jnp.where(picks[r], local + 1.0, 0.0), axis=1, keepdims=True) - 1.0
        meta = jnp.where(sensor == 2 * r, e, meta)
        meta = jnp.where(sensor == 2 * r + 1, l, meta)
    swapped = jnp.where((dest & 1) == 0, pltpu.roll(meta, OWNERS - 1, 0), pltpu.roll(meta, 1, 0))
    meta = jnp.where(sensor < 4, meta, pltpu.roll(swapped, 4, 1))
    msg[pl.ds(16, OWNERS, stride=PITCH), :] = meta
    pick = jnp.concatenate([jnp.where(p, 1.0, 0.0) for p in picks], axis=0).astype(jnp.bfloat16)
    loads[2].wait()
    for j in range(8):
        whole = stage[:, j * 128 : (j + 1) * 128]
        part_a = whole.astype(jnp.bfloat16)
        rest = whole - part_a.astype(jnp.float32)
        part_b = rest.astype(jnp.bfloat16)
        part_c = (rest - part_b.astype(jnp.float32)).astype(jnp.bfloat16)
        out = jnp.dot(pick, part_a, preferred_element_type=jnp.float32)
        out += jnp.dot(pick, part_b, preferred_element_type=jnp.float32)
        out += jnp.dot(pick, part_c, preferred_element_type=jnp.float32)
        msg[pl.ds(j, OWNERS, stride=PITCH), :] = out[:OWNERS]
        msg[pl.ds(8 + j, OWNERS, stride=PITCH), :] = out[OWNERS:]

    for c in field_loads:
        c.wait()

    def fill_faces(values, speeds):
        for k, v in enumerate(values):
            zs[0, 8 * k : 8 * k + 8, :] = v[15]
            zs[1, 8 * k : 8 * k + 8, :] = v[0]
            xs[0, 16 * k : 16 * k + 16, :] = v[:, 7, :]
            xs[1, 16 * k : 16 * k + 16, :] = v[:, 0, :]
            t = v.reshape(128, 128).T
            ys[0, k : k + 1, :] = t[127:128]
            ys[1, k : k + 1, :] = t[0:1]
        if speeds is not None:
            vz, vx, vy = speeds
            zs[0, 16:24, :] = vz[15]
            zs[1, 16:24, :] = vz[0]
            xs[0, 32:48, :] = vx[:, 7, :]
            xs[1, 32:48, :] = vx[:, 0, :]
            t = vy.reshape(128, 128).T
            ys[0, 2:3, :] = t[127:128]
            ys[1, 2:3, :] = t[0:1]

    def face_copies(rnd):
        copies = []
        for d in range(2):
            step = 1 if d == 0 else -1
            for k, (src, dst, dev) in enumerate((
                (zs, zr, (gx, gy, lax.rem(gz + step + N_Z, N_Z))),
                (xs, xr, (lax.rem(gx + step + N_X, N_X), gy, gz)),
                (ys, yr, (gx, lax.rem(gy + step + N_Y, N_Y), gz)),
            )):
                n = src.shape[1]
                if rnd == 1 and k < 2:
                    n = n // 3 * 2
                copies.append(
                    pltpu.make_async_remote_copy(
                        src_ref=src.at[d, pl.ds(0, n)],
                        dst_ref=dst.at[rnd, d, pl.ds(0, n)],
                        send_sem=face_send.at[rnd, d, k],
                        recv_sem=face_recv.at[rnd, d, k],
                        device_id=dev,
                        device_id_type=MESH,
                    )
                )
        return copies

    fill_faces([fields[UP], fields[LO]], [fields[VZ], fields[VX], fields[VY]])

    pl.semaphore_wait(barrier, HALF - 1 + len(others))

    first = face_copies(0)
    for c in first:
        c.start()

    def slot(px, py, row):
        return pl.multiple_of((px * N_Y + py) * PITCH + row, 8)

    def message(i, near, group):
        px, py = peer(i, gx, gy)
        return pltpu.make_async_remote_copy(
            src_ref=msg.at[pl.ds(slot(px, py if near else py ^ 1, 0), ROWS[near])],
            dst_ref=got.at[near * HALF + i, pl.ds(0, ROWS[near])],
            send_sem=send_sem.at[near],
            recv_sem=(near_sem if near else far_sem).at[group],
            device_id=(px, py, gz),
            device_id_type=MESH,
        )

    for near, groups in ((0, FAR), (1, NEAR)):
        for group, (lo, hi) in enumerate(groups):

            def send(i, carry):
                message(i, near, group).start()
                return carry

            lax.fori_loop(lo, hi, send, 0)

    x_of = lax.broadcasted_iota(jnp.int32, (16, 8, 128), 1)
    y_of = lax.broadcasted_iota(jnp.int32, (16, 8, 128), 2)
    inner = [
        (gz > 0, gz < N_Z - 1),
        (gx > 0, gx < N_X - 1),
        (gy > 0, gy < N_Y - 1),
    ]

    def keep(flag, value):
        return jnp.where(flag, value, 0.0)

    def halo(rnd, dim, k, side):
        flag = inner[dim][side]
        if dim == 0:
            return keep(flag, zr[rnd, side, 8 * k : 8 * k + 8, :])[None]
        if dim == 1:
            return keep(flag, xr[rnd, side, 16 * k : 16 * k + 16, :])[:, None, :]
        columns = turned[side][:, k : k + 1]
        return keep(flag, columns).reshape(16, 8, 1)

    def shifted(value, rnd, dim, k):
        below, above = halo(rnd, dim, k, 0), halo(rnd, dim, k, 1)
        if dim == 0:
            return (
                jnp.concatenate([below, value[:15]], axis=0),
                jnp.concatenate([value[1:], above], axis=0),
            )
        if dim == 1:
            return (
                jnp.where(x_of == 0, below, pltpu.roll(value, 1, 1)),
                jnp.where(x_of == 7, above, pltpu.roll(value, 7, 1)),
            )
        return (
            jnp.where(y_of == 0, below, pltpu.roll(value, 1, 2)),
            jnp.where(y_of == 127, above, pltpu.roll(value, 127, 2)),
        )

    turn[...] = jnp.zeros_like(turn)

    def turn_faces(rnd):
        sides = []
        for d in range(2):
            turn[d, 0:8, :] = yr[rnd, d]
            sides.append(turn[d].T)
        return sides

    for c in first:
        c.wait()
    turned = turn_faces(0)
    diff = fields[DIFF]
    centre = 1.0 - 6.0 * diff
    for dim, which in enumerate((VZ, VX, VY)):
        v = fields[which]
        centre = centre - jnp.abs(v)
        v_below, v_above = shifted(v, 0, dim, 2)
        coefs[2 * dim] = jnp.maximum(v_below, 0.0) + diff
        coefs[2 * dim + 1] = jnp.maximum(-v_above, 0.0) + diff
    coefs[6] = centre

    def advance(rnd):
        results = []
        for k in range(2):
            value = fields[k]
            total = coefs[6] * value
            for dim in range(3):
                below, above = shifted(value, rnd, dim, k)
                total = total + coefs[2 * dim] * below + coefs[2 * dim + 1] * above
            results.append(total)
        return results

    once = advance(0)
    fields[UP] = once[0]
    fields[LO] = once[1]
    fill_faces([fields[UP], fields[LO]], None)
    second = face_copies(1)
    for c in second:
        c.start()

    def tables():
        return (
            tuple(ceil_t[b] for b in range(16)),
            tuple(floor_t[b] for b in range(16)),
        )

    def store(t):
        for b in range(16):
            ceil_t[b] = t[0][b]
            floor_t[b] = t[1][b]

    def spread(m, row, near):
        for k in range(4):
            lane = 4 * near + k
            wide[4 * m + k] = jnp.broadcast_to(row[:, lane : lane + 1], (8, 128))

    def take(t, m, rows):
        for r in range(2):
            t = merge(t, rows(r), wide[4 * m + 2 * r], wide[4 * m + 2 * r + 1])
        return t

    def begin(near):
        full = lambda v: jnp.full((8, 128), v, jnp.float32)
        start = (tuple(full(jnp.inf) for _ in range(16)), tuple(full(-jnp.inf) for _ in range(16)))
        py = gy if near else gy ^ 1
        spread(0, msg[pl.ds(slot(gx, gy ^ 1, 16), 8), :][0:1], near)
        store(take(start, 0, lambda r: msg[pl.ds(slot(gx, py, 8 * r), 8), :]))

    def arrived(near, group):
        lo, hi = (NEAR if near else FAR)[group]
        block_of = got.at[pl.ds(near * HALF + lo, hi - lo), pl.ds(0, ROWS[near])]
        return pltpu.make_async_remote_copy(
            src_ref=block_of,
            dst_ref=block_of,
            send_sem=send_sem.at[near],
            recv_sem=(near_sem if near else far_sem).at[group],
            device_id=mirror,
            device_id_type=MESH,
        )

    def await_group(near, group):
        lo, hi = (NEAR if near else FAR)[group]
        n = hi - lo
        arrived(near, group).wait_recv()
        for m in range(n):
            spread(m, got[lo + m, 16:17, :], near)

        def one(m, t):
            return take(t, m, lambda r: got[near * HALF + lo + m, 8 * r : 8 * r + 8, :])

        def body(h, t):
            return one(2 * h + 1, one(2 * h, t))

        t = lax.fori_loop(0, n // 2, body, tables())
        store(one(n - 1, t) if n % 2 else t)

    begin(0)
    for group in range(len(FAR)):
        await_group(0, group)
    relay[0] = ceil_t[...]
    relay[1] = floor_t[...]
    hand_over = pltpu.make_async_remote_copy(
        src_ref=relay,
        dst_ref=relayed,
        send_sem=relay_sem.at[0],
        recv_sem=relay_sem.at[1],
        device_id=mirror,
        device_id_type=MESH,
    )
    hand_over.start()

    for c in second:
        c.wait()
    turned = turn_faces(1)
    twice = advance(1)
    fields[UP] = twice[0]
    fields[LO] = twice[1]

    begin(1)
    for group in range(len(NEAR) - 1):
        await_group(1, group)
    hand_over.wait()
    ceil_t[...] = jnp.minimum(ceil_t[...], relayed[0])
    floor_t[...] = jnp.maximum(floor_t[...], relayed[1])
    await_group(1, len(NEAR) - 1)

    for table, which, out in ((ceil_t, UP, upper_out), (floor_t, LO, lower_out)):
        rows = regroup([table[b] for b in range(16)])
        for g in range(16):
            flat[pl.ds(g, 8, stride=16), :] = rows[g]
        pick_of = jnp.minimum if which == UP else jnp.maximum
        out[...] = pick_of(fields[which], flat[...].reshape(16, 8, 128))

    for near, groups in ((0, FAR), (1, NEAR)):
        for group in range(len(groups)):
            arrived(near, group).wait_send()


def shards(*args):
    f32 = jnp.float32
    dma = pltpu.SemaphoreType.DMA
    return pl.pallas_call(
        kernel,
        out_shape=[jax.ShapeDtypeStruct((16, 8, 128), f32)] * 2,
        in_specs=[pl.BlockSpec(memory_space=pl.ANY)] * 7,
        out_specs=[pl.BlockSpec(memory_space=pltpu.VMEM)] * 2,
        scratch_shapes=[
            pltpu.VMEM((6, 16, 8, 128), f32),
            pltpu.VMEM((7, 16, 8, 128), f32),
            pltpu.VMEM((128, 1024), f32),
            pltpu.VMEM((1, 128), f32),
            pltpu.VMEM((1, 128), jnp.int32),
            pltpu.VMEM((OWNERS * PITCH, 128), f32),
            pltpu.VMEM((OWNERS, PITCH, 128), f32),
            pltpu.VMEM((16, 8, 128), f32),
            pltpu.VMEM((16, 8, 128), f32),
            pltpu.VMEM((128, 128), f32),
            pltpu.VMEM((2, 24, 128), f32),
            pltpu.VMEM((2, 2, 24, 128), f32),
            pltpu.VMEM((2, 48, 128), f32),
            pltpu.VMEM((2, 2, 48, 128), f32),
            pltpu.VMEM((2, 8, 128), f32),
            pltpu.VMEM((2, 2, 8, 128), f32),
            pltpu.VMEM((2, 128, 128), f32),
            pltpu.VMEM((64, 8, 128), f32),
            pltpu.VMEM((2, 16, 8, 128), f32),
            pltpu.VMEM((2, 16, 8, 128), f32),
            dma((4,)),
            dma((3,)),
            dma((2,)),
            dma((len(FAR),)),
            dma((len(NEAR),)),
            dma((2,)),
            dma((2, 2, 3)),
            dma((2, 2, 3)),
        ],
        compiler_params=pltpu.CompilerParams(
            collective_id=0, has_side_effects=True, vmem_limit_bytes=56 << 20
        ),
        cost_estimate=pl.CostEstimate(flops=10**8, bytes_accessed=2 << 20, transcendentals=0),
    )(*args)


def solution(mesh):
    in_specs = (
        P("gz", "gx", "gy"),
        P("gz", "gx", "gy"),
        P(None, "gz", "gx", "gy"),
        P("gz", "gx", "gy"),
        P("gz", ("gx", "gy"), None),
        P("gz", ("gx", "gy")),
        P("gz", ("gx", "gy")),
    )
    out_specs = (P("gz", "gx", "gy"), P("gz", "gx", "gy"))
    return jax.shard_map(shards, mesh=mesh, in_specs=in_specs, out_specs=out_specs, check_vma=False)
```

```python
import jax
import jax.numpy as jnp
from jax import lax
from jax.experimental import pallas as pl
from jax.experimental.pallas import tpu as pltpu
from jax.sharding import PartitionSpec as P

MESH = pl.DeviceIdType.MESH
N_X, N_Y, N_Z = 16, 8, 4
OWNERS = N_X * N_Y
HALF = OWNERS // 2
FAR = ((1, 16), (16, 32), (32, 48), (48, 64))
NEAR = ((1, 16), (16, 32), (32, 48), (48, 60), (60, 64))
ROWS = (17, 16)
PITCH = 24
UP, LO, VZ, VX, VY, DIFF = range(6)


def peer(i, gx, gy):
    along_y = ((gx >> 1) + i) & 7
    core = (gx ^ (i >> 3)) & 1
    return along_y * 2 + core, (gy + 2 * (i >> 4)) & (N_Y - 1)


def lane_of(shape):
    return lax.broadcasted_iota(jnp.int32, shape, len(shape) - 1)


def merge(tables, block, err, label):
    ceilings, floors = tables
    high = block + err
    low = block - err
    new_c, new_f = [], []
    for b in range(16):
        mine = label == float(b)
        new_c.append(jnp.minimum(ceilings[b], jnp.where(mine, high, jnp.inf)))
        new_f.append(jnp.maximum(floors[b], jnp.where(mine, low, -jnp.inf)))
    return tuple(new_c), tuple(new_f)


def regroup(table):
    rows = list(table)
    group = lane_of((8, 128)) // 8
    for k in (1, 2, 4, 8):
        high = lax.rem(group // k, 2) == 1
        for i in range(16):
            if i & k == 0:
                a, b = rows[i], rows[i | k]
                rows[i] = jnp.where(high, pltpu.roll(b, 8 * k, 1), a)
                rows[i | k] = jnp.where(high, b, pltpu.roll(a, 128 - 8 * k, 1))
    return rows


def kernel(
    upper, lower, velocity, diffusivity, center, error, block,
    both_out,
    fields, coefs, stage, err_v, blk_v, msg, got, ceil_t, floor_t, flat,
    zs, zr, xs, xr, ys, yr, turn, wide, relay, relayed,
    in_sem, c_sem, send_sem, far_sem, near_sem, relay_sem, face_send, face_recv,
):
    gx, gy, gz = lax.axis_index("gx"), lax.axis_index("gy"), lax.axis_index("gz")

    loads = [
        pltpu.make_async_copy(error, err_v, c_sem.at[0]),
        pltpu.make_async_copy(block, blk_v, c_sem.at[1]),
        pltpu.make_async_copy(center.at[0], stage, c_sem.at[2]),
    ]
    field_loads = [
        pltpu.make_async_copy(upper, fields.at[UP], in_sem.at[0]),
        pltpu.make_async_copy(lower, fields.at[LO], in_sem.at[1]),
        pltpu.make_async_copy(velocity, fields.at[pl.ds(VZ, 3)], in_sem.at[2]),
        pltpu.make_async_copy(diffusivity, fields.at[DIFF], in_sem.at[3]),
    ]
    for c in loads + field_loads:
        c.start()

    barrier = pltpu.get_barrier_semaphore()

    def greet(i, carry):
        px, py = peer(i, gx, gy)
        pl.semaphore_signal(barrier, inc=1, device_id=(px, py, gz), device_id_type=MESH)
        return carry

    mirror = (gx, gy ^ 1, gz)
    sideways = (gx, (gy + jnp.where((gy & 1) == 0, N_Y - 1, 1)) & (N_Y - 1), gz)
    others = [mirror, sideways] + [(gx, gy, (gz + d) & (N_Z - 1)) for d in (1, N_Z - 1)]
    for dev in others:
        pl.semaphore_signal(barrier, inc=1, device_id=dev, device_id_type=MESH)
    lax.fori_loop(1, HALF, greet, 0)

    loads[0].wait()
    loads[1].wait()
    blk = blk_v[...]
    block_y = jnp.bitwise_and(blk, 127)
    owner = (blk // 128) * N_Y + block_y // 16
    local = jnp.bitwise_and(block_y, 15).astype(jnp.float32)
    dest = lax.broadcasted_iota(jnp.int32, (OWNERS, 128), 0)
    sensor = lane_of((OWNERS, 128))
    goes = jnp.broadcast_to(owner, (OWNERS, 128)) == dest
    before = jnp.where(dest < sensor, 1.0, 0.0).astype(jnp.bfloat16)
    rank = jnp.dot(
        jnp.where(goes, 1.0, 0.0).astype(jnp.bfloat16), before, preferred_element_type=jnp.float32
    )
    picks = [jnp.logical_and(goes, rank < 0.5), jnp.logical_and(goes, rank > 0.5)]
    meta = jnp.full((OWNERS, 128), -1.0, jnp.float32)
    for r in range(2):
        e = jnp.sum(jnp.where(picks[r], err_v[...], 0.0), axis=1, keepdims=True)
        l = jnp.sum(jnp.where(picks[r], local + 1.0, 0.0), axis=1, keepdims=True) - 1.0
        meta = jnp.where(sensor == 2 * r, e, meta)
        meta = jnp.where(sensor == 2 * r + 1, l, meta)
    swapped = jnp.where((dest & 1) == 0, pltpu.roll(meta, OWNERS - 1, 0), pltpu.roll(meta, 1, 0))
    meta = jnp.where(sensor < 4, meta, pltpu.roll(swapped, 4, 1))
    msg[pl.ds(16, OWNERS, stride=PITCH), :] = meta
    pick = jnp.concatenate([jnp.where(p, 1.0, 0.0) for p in picks], axis=0).astype(jnp.bfloat16)
    loads[2].wait()
    for j in range(8):
        whole = stage[:, j * 128 : (j + 1) * 128]
        part_a = whole.astype(jnp.bfloat16)
        rest = whole - part_a.astype(jnp.float32)
        part_b = rest.astype(jnp.bfloat16)
        part_c = (rest - part_b.astype(jnp.float32)).astype(jnp.bfloat16)
        out = jnp.dot(pick, part_a, preferred_element_type=jnp.float32)
        out += jnp.dot(pick, part_b, preferred_element_type=jnp.float32)
        out += jnp.dot(pick, part_c, preferred_element_type=jnp.float32)
        msg[pl.ds(j, OWNERS, stride=PITCH), :] = out[:OWNERS]
        msg[pl.ds(8 + j, OWNERS, stride=PITCH), :] = out[OWNERS:]

    for c in field_loads:
        c.wait()

    def fill_faces(values, speeds):
        for k, v in enumerate(values):
            zs[0, 8 * k : 8 * k + 8, :] = v[15]
            zs[1, 8 * k : 8 * k + 8, :] = v[0]
            xs[0, 16 * k : 16 * k + 16, :] = v[:, 7, :]
            xs[1, 16 * k : 16 * k + 16, :] = v[:, 0, :]
            t = v.reshape(128, 128).T
            ys[0, k : k + 1, :] = t[127:128]
            ys[1, k : k + 1, :] = t[0:1]
        if speeds is not None:
            vz, vx, vy = speeds
            zs[0, 16:24, :] = vz[15]
            zs[1, 16:24, :] = vz[0]
            xs[0, 32:48, :] = vx[:, 7, :]
            xs[1, 32:48, :] = vx[:, 0, :]
            t = vy.reshape(128, 128).T
            ys[0, 2:3, :] = t[127:128]
            ys[1, 2:3, :] = t[0:1]

    def face_copies(rnd):
        copies = []
        for d in range(2):
            step = 1 if d == 0 else -1
            for k, (src, dst, dev) in enumerate((
                (zs, zr, (gx, gy, lax.rem(gz + step + N_Z, N_Z))),
                (xs, xr, (lax.rem(gx + step + N_X, N_X), gy, gz)),
                (ys, yr, (gx, lax.rem(gy + step + N_Y, N_Y), gz)),
            )):
                n = src.shape[1]
                if rnd == 1 and k < 2:
                    n = n // 3 * 2
                copies.append(
                    pltpu.make_async_remote_copy(
                        src_ref=src.at[d, pl.ds(0, n)],
                        dst_ref=dst.at[rnd, d, pl.ds(0, n)],
                        send_sem=face_send.at[rnd, d, k],
                        recv_sem=face_recv.at[rnd, d, k],
                        device_id=dev,
                        device_id_type=MESH,
                    )
                )
        return copies

    fill_faces([fields[UP], fields[LO]], [fields[VZ], fields[VX], fields[VY]])

    pl.semaphore_wait(barrier, HALF - 1 + len(others))

    first = face_copies(0)
    for c in first:
        c.start()

    def slot(px, py, row):
        return pl.multiple_of((px * N_Y + py) * PITCH + row, 8)

    def message(i, near, group):
        px, py = peer(i, gx, gy)
        return pltpu.make_async_remote_copy(
            src_ref=msg.at[pl.ds(slot(px, py if near else py ^ 1, 0), ROWS[near])],
            dst_ref=got.at[near * HALF + i, pl.ds(0, ROWS[near])],
            send_sem=send_sem.at[near],
            recv_sem=(near_sem if near else far_sem).at[group],
            device_id=(px, py, gz),
            device_id_type=MESH,
        )

    for near, groups in ((0, FAR), (1, NEAR)):
        for group, (lo, hi) in enumerate(groups):

            def send(i, carry):
                message(i, near, group).start()
                return carry

            lax.fori_loop(lo, hi, send, 0)

    x_of = lax.broadcasted_iota(jnp.int32, (16, 8, 128), 1)
    y_of = lax.broadcasted_iota(jnp.int32, (16, 8, 128), 2)
    inner = [
        (gz > 0, gz < N_Z - 1),
        (gx > 0, gx < N_X - 1),
        (gy > 0, gy < N_Y - 1),
    ]

    def keep(flag, value):
        return jnp.where(flag, value, 0.0)

    def halo(rnd, dim, k, side):
        flag = inner[dim][side]
        if dim == 0:
            return keep(flag, zr[rnd, side, 8 * k : 8 * k + 8, :])[None]
        if dim == 1:
            return keep(flag, xr[rnd, side, 16 * k : 16 * k + 16, :])[:, None, :]
        columns = turned[side][:, k : k + 1]
        return keep(flag, columns).reshape(16, 8, 1)

    def shifted(value, rnd, dim, k):
        below, above = halo(rnd, dim, k, 0), halo(rnd, dim, k, 1)
        if dim == 0:
            return (
                jnp.concatenate([below, value[:15]], axis=0),
                jnp.concatenate([value[1:], above], axis=0),
            )
        if dim == 1:
            return (
                jnp.where(x_of == 0, below, pltpu.roll(value, 1, 1)),
                jnp.where(x_of == 7, above, pltpu.roll(value, 7, 1)),
            )
        return (
            jnp.where(y_of == 0, below, pltpu.roll(value, 1, 2)),
            jnp.where(y_of == 127, above, pltpu.roll(value, 127, 2)),
        )

    turn[...] = jnp.zeros_like(turn)

    def turn_faces(rnd):
        sides = []
        for d in range(2):
            turn[d, 0:8, :] = yr[rnd, d]
            sides.append(turn[d].T)
        return sides

    for c in first:
        c.wait()
    turned = turn_faces(0)
    diff = fields[DIFF]
    centre = 1.0 - 6.0 * diff
    for dim, which in enumerate((VZ, VX, VY)):
        v = fields[which]
        centre = centre - jnp.abs(v)
        v_below, v_above = shifted(v, 0, dim, 2)
        coefs[2 * dim] = jnp.maximum(v_below, 0.0) + diff
        coefs[2 * dim + 1] = jnp.maximum(-v_above, 0.0) + diff
    coefs[6] = centre

    def advance(rnd):
        results = []
        for k in range(2):
            value = fields[k]
            total = coefs[6] * value
            for dim in range(3):
                below, above = shifted(value, rnd, dim, k)
                total = total + coefs[2 * dim] * below + coefs[2 * dim + 1] * above
            results.append(total)
        return results

    once = advance(0)
    fields[UP] = once[0]
    fields[LO] = once[1]
    fill_faces([fields[UP], fields[LO]], None)
    second = face_copies(1)
    for c in second:
        c.start()

    def tables():
        return (
            tuple(ceil_t[b] for b in range(16)),
            tuple(floor_t[b] for b in range(16)),
        )

    def store(t):
        for b in range(16):
            ceil_t[b] = t[0][b]
            floor_t[b] = t[1][b]

    def spread(m, row, near):
        for k in range(4):
            lane = 4 * near + k
            wide[4 * m + k] = jnp.broadcast_to(row[:, lane : lane + 1], (8, 128))

    def take(t, m, rows):
        for r in range(2):
            t = merge(t, rows(r), wide[4 * m + 2 * r], wide[4 * m + 2 * r + 1])
        return t

    def begin(near):
        full = lambda v: jnp.full((8, 128), v, jnp.float32)
        start = (tuple(full(jnp.inf) for _ in range(16)), tuple(full(-jnp.inf) for _ in range(16)))
        py = gy if near else gy ^ 1
        spread(0, msg[pl.ds(slot(gx, gy ^ 1, 16), 8), :][0:1], near)
        store(take(start, 0, lambda r: msg[pl.ds(slot(gx, py, 8 * r), 8), :]))

    def arrived(near, group):
        lo, hi = (NEAR if near else FAR)[group]
        block_of = got.at[pl.ds(near * HALF + lo, hi - lo), pl.ds(0, ROWS[near])]
        return pltpu.make_async_remote_copy(
            src_ref=block_of,
            dst_ref=block_of,
            send_sem=send_sem.at[near],
            recv_sem=(near_sem if near else far_sem).at[group],
            device_id=mirror,
            device_id_type=MESH,
        )

    def await_group(near, group):
        lo, hi = (NEAR if near else FAR)[group]
        n = hi - lo
        arrived(near, group).wait_recv()
        for m in range(n):
            spread(m, got[lo + m, 16:17, :], near)

        def one(m, t):
            return take(t, m, lambda r: got[near * HALF + lo + m, 8 * r : 8 * r + 8, :])

        def body(h, t):
            return one(2 * h + 1, one(2 * h, t))

        t = lax.fori_loop(0, n // 2, body, tables())
        store(one(n - 1, t) if n % 2 else t)

    begin(0)
    for group in range(len(FAR)):
        await_group(0, group)
    relay[0] = ceil_t[...]
    relay[1] = floor_t[...]
    hand_over = pltpu.make_async_remote_copy(
        src_ref=relay,
        dst_ref=relayed,
        send_sem=relay_sem.at[0],
        recv_sem=relay_sem.at[1],
        device_id=mirror,
        device_id_type=MESH,
    )
    hand_over.start()

    for c in second:
        c.wait()
    turned = turn_faces(1)
    twice = advance(1)
    fields[UP] = twice[0]
    fields[LO] = twice[1]

    begin(1)
    for group in range(len(NEAR) - 1):
        await_group(1, group)
    hand_over.wait()
    ceil_t[...] = jnp.minimum(ceil_t[...], relayed[0])
    floor_t[...] = jnp.maximum(floor_t[...], relayed[1])
    await_group(1, len(NEAR) - 1)

    for table, which, out in ((ceil_t, UP, both_out.at[0]), (floor_t, LO, both_out.at[1])):
        rows = regroup([table[b] for b in range(16)])
        for g in range(16):
            flat[pl.ds(g, 8, stride=16), :] = rows[g]
        pick_of = jnp.minimum if which == UP else jnp.maximum
        out[...] = pick_of(fields[which], flat[...].reshape(16, 8, 128))

    for near, groups in ((0, FAR), (1, NEAR)):
        for group in range(len(groups)):
            arrived(near, group).wait_send()


def shards(*args):
    f32 = jnp.float32
    dma = pltpu.SemaphoreType.DMA
    both = pl.pallas_call(
        kernel,
        out_shape=pltpu.VMEM((2, 16, 8, 128), f32),
        in_specs=[pl.BlockSpec(memory_space=pl.ANY)] * 7,
        out_specs=pl.BlockSpec(memory_space=pltpu.VMEM),
        scratch_shapes=[
            pltpu.VMEM((6, 16, 8, 128), f32),
            pltpu.VMEM((7, 16, 8, 128), f32),
            pltpu.VMEM((128, 1024), f32),
            pltpu.VMEM((1, 128), f32),
            pltpu.VMEM((1, 128), jnp.int32),
            pltpu.VMEM((OWNERS * PITCH, 128), f32),
            pltpu.VMEM((OWNERS, PITCH, 128), f32),
            pltpu.VMEM((16, 8, 128), f32),
            pltpu.VMEM((16, 8, 128), f32),
            pltpu.VMEM((128, 128), f32),
            pltpu.VMEM((2, 24, 128), f32),
            pltpu.VMEM((2, 2, 24, 128), f32),
            pltpu.VMEM((2, 48, 128), f32),
            pltpu.VMEM((2, 2, 48, 128), f32),
            pltpu.VMEM((2, 8, 128), f32),
            pltpu.VMEM((2, 2, 8, 128), f32),
            pltpu.VMEM((2, 128, 128), f32),
            pltpu.VMEM((64, 8, 128), f32),
            pltpu.VMEM((2, 16, 8, 128), f32),
            pltpu.VMEM((2, 16, 8, 128), f32),
            dma((4,)),
            dma((3,)),
            dma((2,)),
            dma((len(FAR),)),
            dma((len(NEAR),)),
            dma((2,)),
            dma((2, 2, 3)),
            dma((2, 2, 3)),
        ],
        compiler_params=pltpu.CompilerParams(
            collective_id=0, has_side_effects=True, vmem_limit_bytes=32 << 20
        ),
        cost_estimate=pl.CostEstimate(flops=10**8, bytes_accessed=2 << 20, transcendentals=0),
    )(*[pltpu.with_memory_space_constraint(a, pltpu.HBM) for a in args])
    return both[0], both[1]


def solution(mesh):
    in_specs = (
        P("gz", "gx", "gy"),
        P("gz", "gx", "gy"),
        P(None, "gz", "gx", "gy"),
        P("gz", "gx", "gy"),
        P("gz", ("gx", "gy"), None),
        P("gz", ("gx", "gy")),
        P("gz", ("gx", "gy")),
    )
    out_specs = (P("gz", "gx", "gy"), P("gz", "gx", "gy"))
    return jax.shard_map(shards, mesh=mesh, in_specs=in_specs, out_specs=out_specs, check_vma=False)
```

```python
import jax
import jax.numpy as jnp
from jax import lax
from jax.experimental import pallas as pl
from jax.experimental.pallas import tpu as pltpu
from jax.sharding import PartitionSpec as P

MESH = pl.DeviceIdType.MESH
N_X, N_Y, N_Z = 16, 8, 4
OWNERS = N_X * N_Y
HALF = OWNERS // 2
FAR = ((1, 16), (16, 32), (32, 48), (48, 64))
NEAR = ((1, 16), (16, 32), (32, 48), (48, 60), (60, 64))
PART = ((8, 9), (0, 8))
WHOLE = (0, 16)
ROW = (8, 0)
PITCH = 24
UP, LO, VZ, VX, VY, DIFF = range(6)


def peer(i, gx, gy):
    along_y = ((gx >> 1) + i) & 7
    core = (gx ^ (i >> 3)) & 1
    return along_y * 2 + core, (gy + 2 * (i >> 4)) & (N_Y - 1)


def lane_of(shape):
    return lax.broadcasted_iota(jnp.int32, shape, len(shape) - 1)


def merge(tables, block, err, label):
    ceilings, floors = tables
    high = block + err
    low = block - err
    new_c, new_f = [], []
    for b in range(16):
        mine = label == float(b)
        new_c.append(jnp.minimum(ceilings[b], jnp.where(mine, high, jnp.inf)))
        new_f.append(jnp.maximum(floors[b], jnp.where(mine, low, -jnp.inf)))
    return tuple(new_c), tuple(new_f)


def regroup(table):
    rows = list(table)
    group = lane_of((8, 128)) // 8
    for k in (1, 2, 4, 8):
        high = lax.rem(group // k, 2) == 1
        for i in range(16):
            if i & k == 0:
                a, b = rows[i], rows[i | k]
                rows[i] = jnp.where(high, pltpu.roll(b, 8 * k, 1), a)
                rows[i | k] = jnp.where(high, b, pltpu.roll(a, 128 - 8 * k, 1))
    return rows


def kernel(
    upper, lower, velocity, diffusivity, center, error, block,
    both_out,
    fields, coefs, stage, err_v, blk_v, msg, got, tabs, flat,
    zs, zr, xs, xr, ys, yr, turn, wide, relay, relayed,
    in_sem, c_sem, send_sem, arrive_sem, relay_sem, face_send, face_recv, answer_sem,
):
    gx, gy, gz = lax.axis_index("gx"), lax.axis_index("gy"), lax.axis_index("gz")

    loads = [
        pltpu.make_async_copy(error, err_v, c_sem.at[0]),
        pltpu.make_async_copy(block, blk_v, c_sem.at[1]),
        pltpu.make_async_copy(center.at[0], stage, c_sem.at[2]),
    ]
    field_loads = [
        pltpu.make_async_copy(upper, fields.at[UP], in_sem.at[0]),
        pltpu.make_async_copy(lower, fields.at[LO], in_sem.at[1]),
        pltpu.make_async_copy(velocity, fields.at[pl.ds(VZ, 3)], in_sem.at[2]),
        pltpu.make_async_copy(diffusivity, fields.at[DIFF], in_sem.at[3]),
    ]
    for c in loads + field_loads:
        c.start()

    barrier = pltpu.get_barrier_semaphore()

    def greet(i, carry):
        px, py = peer(i, gx, gy)
        pl.semaphore_signal(barrier, inc=1, device_id=(px, py, gz), device_id_type=MESH)
        return carry

    first_half = (gy & 1) == 0
    mirror = (gx, gy ^ 1, gz)
    sideways = (gx, (gy + jnp.where(first_half, N_Y - 1, 1)) & (N_Y - 1), gz)
    above, below = (gx, gy, (gz + 1) & (N_Z - 1)), (gx, gy, (gz + N_Z - 1) & (N_Z - 1))
    last = gz == N_Z - 1
    bottom = gz == 0
    greets = [(first_half, mirror), (first_half, sideways), (gz < N_Z - 1, above), (bottom, below)]
    answers = [
        (jnp.logical_not(first_half), mirror, 0),
        (jnp.logical_not(first_half), sideways, 1),
        (gz > 0, below, 2),
        (last, above, 3),
    ]

    def tell(when, sem, dev):
        @pl.when(when)
        def _():
            pl.semaphore_signal(sem, inc=1, device_id=dev, device_id_type=MESH)

    lax.fori_loop(1, HALF, greet, 0)
    for when, dev in greets:
        tell(when, barrier, dev)

    loads[0].wait()
    loads[1].wait()
    blk = blk_v[...]
    block_y = jnp.bitwise_and(blk, 127)
    owner = (blk // 128) * N_Y + block_y // 16
    local = jnp.bitwise_and(block_y, 15).astype(jnp.float32)
    dest = lax.broadcasted_iota(jnp.int32, (OWNERS, 128), 0)
    sensor = lane_of((OWNERS, 128))
    goes = jnp.broadcast_to(owner, (OWNERS, 128)) == dest
    before = jnp.where(dest < sensor, 1.0, 0.0).astype(jnp.bfloat16)
    rank = jnp.dot(
        jnp.where(goes, 1.0, 0.0).astype(jnp.bfloat16), before, preferred_element_type=jnp.float32
    )
    picks = [jnp.logical_and(goes, rank < 0.5), jnp.logical_and(goes, rank > 0.5)]
    meta = jnp.full((OWNERS, 128), -1.0, jnp.float32)
    for r in range(2):
        e = jnp.sum(jnp.where(picks[r], err_v[...], 0.0), axis=1, keepdims=True)
        l = jnp.sum(jnp.where(picks[r], local + 1.0, 0.0), axis=1, keepdims=True) - 1.0
        meta = jnp.where(sensor == 2 * r, e, meta)
        meta = jnp.where(sensor == 2 * r + 1, l, meta)
    swapped = jnp.where((dest & 1) == 0, pltpu.roll(meta, OWNERS - 1, 0), pltpu.roll(meta, 1, 0))
    meta = jnp.where(sensor < 4, meta, pltpu.roll(swapped, 4, 1))
    msg[pl.ds(16, OWNERS, stride=PITCH), :] = meta
    pick = jnp.concatenate([jnp.where(p, 1.0, 0.0) for p in picks], axis=0).astype(jnp.bfloat16)
    loads[2].wait()
    for j in range(8):
        whole = stage[:, j * 128 : (j + 1) * 128]
        part_a = whole.astype(jnp.bfloat16)
        rest = whole - part_a.astype(jnp.float32)
        part_b = rest.astype(jnp.bfloat16)
        part_c = (rest - part_b.astype(jnp.float32)).astype(jnp.bfloat16)
        out = jnp.dot(pick, part_a, preferred_element_type=jnp.float32)
        out += jnp.dot(pick, part_b, preferred_element_type=jnp.float32)
        out += jnp.dot(pick, part_c, preferred_element_type=jnp.float32)
        at = ROW[j // 4] + j % 4
        msg[pl.ds(at, OWNERS, stride=PITCH), :] = out[:OWNERS]
        msg[pl.ds(at + 4, OWNERS, stride=PITCH), :] = out[OWNERS:]

    for c in field_loads:
        c.wait()

    def fill_faces(values, speeds):
        for k, v in enumerate(values):
            zs[0, 8 * k : 8 * k + 8, :] = v[15]
            zs[1, 8 * k : 8 * k + 8, :] = v[0]
            xs[0, 16 * k : 16 * k + 16, :] = v[:, 7, :]
            xs[1, 16 * k : 16 * k + 16, :] = v[:, 0, :]
            t = v.reshape(128, 128).T
            ys[0, k : k + 1, :] = t[127:128]
            ys[1, k : k + 1, :] = t[0:1]
        if speeds is not None:
            vz, vx, vy = speeds
            zs[0, 16:24, :] = vz[15]
            zs[1, 16:24, :] = vz[0]
            xs[0, 32:48, :] = vx[:, 7, :]
            xs[1, 32:48, :] = vx[:, 0, :]
            t = vy.reshape(128, 128).T
            ys[0, 2:3, :] = t[127:128]
            ys[1, 2:3, :] = t[0:1]

    def face_copies(rnd):
        copies = []
        for d in range(2):
            step = 1 if d == 0 else -1
            for k, (src, dst, dev) in enumerate((
                (zs, zr, (gx, gy, lax.rem(gz + step + N_Z, N_Z))),
                (xs, xr, (lax.rem(gx + step + N_X, N_X), gy, gz)),
                (ys, yr, (gx, lax.rem(gy + step + N_Y, N_Y), gz)),
            )):
                n = src.shape[1]
                if rnd == 1 and k < 2:
                    n = n // 3 * 2
                copies.append(
                    pltpu.make_async_remote_copy(
                        src_ref=src.at[d, pl.ds(0, n)],
                        dst_ref=dst.at[rnd, d, pl.ds(0, n)],
                        send_sem=face_send.at[rnd, d, k],
                        recv_sem=face_recv.at[rnd, d, k],
                        device_id=dev,
                        device_id_type=MESH,
                    )
                )
        return copies

    fill_faces([fields[UP], fields[LO]], [fields[VZ], fields[VX], fields[VY]])

    greeted = sum(jnp.where(when, 1, 0) for when, _, _ in answers)
    pl.semaphore_wait(barrier, HALF - 1 + greeted)
    for when, dev, k in answers:
        tell(when, answer_sem.at[k], dev)

    def slot(px, py, row):
        return pl.multiple_of((px * N_Y + py) * PITCH + row, 8)

    def groups_of(phase):
        return NEAR if phase == 2 else FAR

    def rows_of(phase):
        return WHOLE if phase == 2 else PART[phase]

    def message(i, phase, group):
        px, py = peer(i, gx, gy)
        near = phase // 2
        row, rows = rows_of(phase)
        return pltpu.make_async_remote_copy(
            src_ref=msg.at[pl.ds(slot(px, py if near else py ^ 1, row), rows)],
            dst_ref=got.at[near * HALF + i, pl.ds(row, rows)],
            send_sem=send_sem.at[phase],
            recv_sem=arrive_sem.at[phase, group],
            device_id=(px, py, gz),
            device_id_type=MESH,
        )

    def send_groups(phase):
        for group, (lo, hi) in enumerate(groups_of(phase)):

            def body(i, carry):
                message(i, phase, group).start()
                return carry

            lax.fori_loop(lo, hi, body, 0)

    send_groups(0)
    send_groups(1)

    for k, (when, _) in enumerate(greets):

        @pl.when(when)
        def _():
            pl.semaphore_wait(answer_sem.at[k], 1)

    first = face_copies(0)
    for c in first:
        c.start()
    send_groups(2)

    x_of = lax.broadcasted_iota(jnp.int32, (16, 8, 128), 1)
    y_of = lax.broadcasted_iota(jnp.int32, (16, 8, 128), 2)
    inner = [
        (gz > 0, gz < N_Z - 1),
        (gx > 0, gx < N_X - 1),
        (gy > 0, gy < N_Y - 1),
    ]

    def keep(flag, value):
        return jnp.where(flag, value, 0.0)

    def halo(rnd, dim, k, side):
        flag = inner[dim][side]
        if dim == 0:
            return keep(flag, zr[rnd, side, 8 * k : 8 * k + 8, :])[None]
        if dim == 1:
            return keep(flag, xr[rnd, side, 16 * k : 16 * k + 16, :])[:, None, :]
        columns = turned[side][:, k : k + 1]
        return keep(flag, columns).reshape(16, 8, 1)

    def shifted(value, rnd, dim, k):
        below, above = halo(rnd, dim, k, 0), halo(rnd, dim, k, 1)
        if dim == 0:
            return (
                jnp.concatenate([below, value[:15]], axis=0),
                jnp.concatenate([value[1:], above], axis=0),
            )
        if dim == 1:
            return (
                jnp.where(x_of == 0, below, pltpu.roll(value, 1, 1)),
                jnp.where(x_of == 7, above, pltpu.roll(value, 7, 1)),
            )
        return (
            jnp.where(y_of == 0, below, pltpu.roll(value, 1, 2)),
            jnp.where(y_of == 127, above, pltpu.roll(value, 127, 2)),
        )

    turn[...] = jnp.zeros_like(turn)

    def turn_faces(rnd):
        sides = []
        for d in range(2):
            turn[d, 0:8, :] = yr[rnd, d]
            sides.append(turn[d].T)
        return sides

    upper_rows = lax.broadcasted_iota(jnp.int32, (8, 128), 0) < 4
    full = lambda v: jnp.full((8, 128), v, jnp.float32)
    nothing = (full(jnp.inf), full(-jnp.inf))
    pick_of = (jnp.minimum, jnp.maximum)

    def tables(part):
        return tuple(tuple(tabs[part, kind, b] for b in range(16)) for kind in range(2))

    def store(part, t):
        for kind in range(2):
            for b in range(16):
                tabs[part, kind, b] = t[kind][b]

    def spread(m, row, near):
        for k in range(2):
            a, b = (
                jnp.broadcast_to(row[:, lane : lane + 1], (8, 128))
                for lane in (4 * near + k, 4 * near + k + 2)
            )
            wide[2 * m + k] = jnp.where(upper_rows, a, b)

    def begin(near):
        py = gy if near else gy ^ 1
        spread(0, msg[pl.ds(slot(gx, gy ^ 1, 16), 8), :][0:1], near)
        start = tuple((nothing[kind],) * 16 for kind in range(2))
        for part in range(2):
            store(part, merge(start, msg[pl.ds(slot(gx, py, ROW[part]), 8), :], wide[0], wide[1]))

    def arrived(phase, group):
        lo, hi = groups_of(phase)[group]
        row, rows = rows_of(phase)
        block_of = got.at[pl.ds(phase // 2 * HALF + lo, hi - lo), pl.ds(row, rows)]
        return pltpu.make_async_remote_copy(
            src_ref=block_of,
            dst_ref=block_of,
            send_sem=send_sem.at[phase],
            recv_sem=arrive_sem.at[phase, group],
            device_id=mirror,
            device_id_type=MESH,
        )

    def await_group(phase, group):
        near = phase // 2
        lo, hi = groups_of(phase)[group]
        n = hi - lo
        arrived(phase, group).wait_recv()
        for m in range(n):
            spread(m, got[lo + m, 16:17, :], near)
        for part in (0, 1) if near else (phase,):

            def one(m, t):
                rows = got[near * HALF + lo + m, ROW[part] : ROW[part] + 8, :]
                return merge(t, rows, wide[2 * m], wide[2 * m + 1])

            def body(h, t):
                return one(2 * h + 1, one(2 * h, t))

            t = lax.fori_loop(0, n // 2, body, tables(part))
            store(part, one(n - 1, t) if n % 2 else t)

    def folded(part, kind, b):
        t = tabs[part, kind, b]
        return pick_of[kind](t, pltpu.roll(t, 4, 0))

    def hand_over(part):
        return pltpu.make_async_remote_copy(
            src_ref=relay.at[part],
            dst_ref=relayed.at[part],
            send_sem=relay_sem.at[0, part],
            recv_sem=relay_sem.at[1, part],
            device_id=mirror,
            device_id_type=MESH,
        )

    def far_part(part):
        for group in range(len(FAR)):
            await_group(part, group)
        for kind in range(2):
            for b in range(8):
                relay[part, kind, b] = jnp.where(
                    upper_rows, folded(part, kind, b), folded(part, kind, b + 8)
                )
        hand_over(part).start()

    begin(0)
    far_part(0)

    for c in first:
        c.wait()
    turned = turn_faces(0)
    diff = fields[DIFF]
    centre = 1.0 - 6.0 * diff
    for dim, which in enumerate((VZ, VX, VY)):
        v = fields[which]
        centre = centre - jnp.abs(v)
        v_below, v_above = shifted(v, 0, dim, 2)
        coefs[2 * dim] = jnp.maximum(v_below, 0.0) + diff
        coefs[2 * dim + 1] = jnp.maximum(-v_above, 0.0) + diff
    coefs[6] = centre

    def advance(rnd):
        results = []
        for k in range(2):
            value = fields[k]
            total = coefs[6] * value
            for dim in range(3):
                below, above = shifted(value, rnd, dim, k)
                total = total + coefs[2 * dim] * below + coefs[2 * dim + 1] * above
            results.append(total)
        return results

    once = advance(0)
    fields[UP] = once[0]
    fields[LO] = once[1]
    fill_faces([fields[UP], fields[LO]], None)
    second = face_copies(1)
    for c in second:
        c.start()

    far_part(1)

    for c in second:
        c.wait()
    turned = turn_faces(1)
    twice = advance(1)
    fields[UP] = twice[0]
    fields[LO] = twice[1]

    begin(1)
    for group in range(len(NEAR) - 1):
        await_group(2, group)
    for part in range(2):
        hand_over(part).wait_recv()
        for kind in range(2):
            for b in range(8):
                came = relayed[part, kind, b]
                for block_at, where in ((b, upper_rows), (b + 8, jnp.logical_not(upper_rows))):
                    tabs[part, kind, block_at] = pick_of[kind](
                        tabs[part, kind, block_at], jnp.where(where, came, nothing[kind])
                    )
    await_group(2, len(NEAR) - 1)

    for kind, (which, out) in enumerate(((UP, both_out.at[0]), (LO, both_out.at[1]))):
        rows = regroup(
            [jnp.where(upper_rows, folded(0, kind, b), folded(1, kind, b)) for b in range(16)]
        )
        for g in range(16):
            flat[pl.ds(g, 8, stride=16), :] = rows[g]
        out[...] = pick_of[kind](fields[which], flat[...].reshape(16, 8, 128))

    for phase in range(3):
        for group in range(len(groups_of(phase))):
            arrived(phase, group).wait_send()
    for part in range(2):
        hand_over(part).wait_send()


def shards(*args):
    f32 = jnp.float32
    dma = pltpu.SemaphoreType.DMA
    both = pl.pallas_call(
        kernel,
        out_shape=pltpu.VMEM((2, 16, 8, 128), f32),
        in_specs=[pl.BlockSpec(memory_space=pl.ANY)] * 7,
        out_specs=pl.BlockSpec(memory_space=pltpu.VMEM),
        scratch_shapes=[
            pltpu.VMEM((6, 16, 8, 128), f32),
            pltpu.VMEM((7, 16, 8, 128), f32),
            pltpu.VMEM((128, 1024), f32),
            pltpu.VMEM((1, 128), f32),
            pltpu.VMEM((1, 128), jnp.int32),
            pltpu.VMEM((OWNERS * PITCH, 128), f32),
            pltpu.VMEM((OWNERS, PITCH, 128), f32),
            pltpu.VMEM((2, 2, 16, 8, 128), f32),
            pltpu.VMEM((128, 128), f32),
            pltpu.VMEM((2, 24, 128), f32),
            pltpu.VMEM((2, 2, 24, 128), f32),
            pltpu.VMEM((2, 48, 128), f32),
            pltpu.VMEM((2, 2, 48, 128), f32),
            pltpu.VMEM((2, 8, 128), f32),
            pltpu.VMEM((2, 2, 8, 128), f32),
            pltpu.VMEM((2, 128, 128), f32),
            pltpu.VMEM((64, 8, 128), f32),
            pltpu.VMEM((2, 2, 8, 8, 128), f32),
            pltpu.VMEM((2, 2, 8, 8, 128), f32),
            dma((4,)),
            dma((3,)),
            dma((3,)),
            dma((3, len(NEAR))),
            dma((2, 2)),
            dma((2, 2, 3)),
            dma((2, 2, 3)),
            pltpu.SemaphoreType.REGULAR((4,)),
        ],
        compiler_params=pltpu.CompilerParams(
            collective_id=0, has_side_effects=True, vmem_limit_bytes=32 << 20
        ),
        cost_estimate=pl.CostEstimate(flops=10**8, bytes_accessed=2 << 20, transcendentals=0),
    )(*[pltpu.with_memory_space_constraint(a, pltpu.HBM) for a in args])
    return both[0], both[1]


def solution(mesh):
    in_specs = (
        P("gz", "gx", "gy"),
        P("gz", "gx", "gy"),
        P(None, "gz", "gx", "gy"),
        P("gz", "gx", "gy"),
        P("gz", ("gx", "gy"), None),
        P("gz", ("gx", "gy")),
        P("gz", ("gx", "gy")),
    )
    out_specs = (P("gz", "gx", "gy"), P("gz", "gx", "gy"))
    return jax.shard_map(shards, mesh=mesh, in_specs=in_specs, out_specs=out_specs, check_vma=False)
```

```python
import jax
import jax.numpy as jnp
from jax import lax
from jax.experimental import pallas as pl
from jax.experimental.pallas import tpu as pltpu
from jax.sharding import PartitionSpec as P

MESH = pl.DeviceIdType.MESH
N_X, N_Y, N_Z = 16, 8, 4
OWNERS = N_X * N_Y
HALF = OWNERS // 2
FAR = ((1, 16), (16, 32), (32, 48), (48, 64))
NEAR = ((1, 16), (16, 32), (32, 48), (48, 60), (60, 64))
PART = ((8, 9), (0, 8))
WHOLE = (0, 16)
ROW = (8, 0)
STEP_AFTER = 3
PITCH = 24
UP, LO, VZ, VX, VY, DIFF = range(6)


def peer(i, gx, gy):
    along_y = ((gx >> 1) + i) & 7
    core = (gx ^ (i >> 3)) & 1
    return along_y * 2 + core, (gy + 2 * (i >> 4)) & (N_Y - 1)


def lane_of(shape):
    return lax.broadcasted_iota(jnp.int32, shape, len(shape) - 1)


def merge(tables, block, err, label):
    ceilings, floors = tables
    high = block + err
    low = block - err
    new_c, new_f = [], []
    for b in range(16):
        mine = label == float(b)
        new_c.append(jnp.minimum(ceilings[b], jnp.where(mine, high, jnp.inf)))
        new_f.append(jnp.maximum(floors[b], jnp.where(mine, low, -jnp.inf)))
    return tuple(new_c), tuple(new_f)


def regroup(table):
    rows = list(table)
    group = lane_of((8, 128)) // 8
    for k in (1, 2, 4, 8):
        high = lax.rem(group // k, 2) == 1
        for i in range(16):
            if i & k == 0:
                a, b = rows[i], rows[i | k]
                rows[i] = jnp.where(high, pltpu.roll(b, 8 * k, 1), a)
                rows[i | k] = jnp.where(high, b, pltpu.roll(a, 128 - 8 * k, 1))
    return rows


def kernel(
    upper, lower, velocity, diffusivity, center, error, block,
    both_out,
    fields, coefs, stage, err_v, blk_v, msg, got, tabs, flat,
    zs, zr, xs, xr, ys, yr, turn, wide, relay, relayed,
    in_sem, c_sem, send_sem, arrive_sem, relay_sem, face_send, face_recv, answer_sem, row_sem,
):
    gx, gy, gz = lax.axis_index("gx"), lax.axis_index("gy"), lax.axis_index("gz")

    loads = [
        pltpu.make_async_copy(error, err_v, c_sem.at[0]),
        pltpu.make_async_copy(block, blk_v, c_sem.at[1]),
        pltpu.make_async_copy(center.at[0], stage, c_sem.at[2]),
    ]
    field_loads = [
        pltpu.make_async_copy(upper, fields.at[UP], in_sem.at[0]),
        pltpu.make_async_copy(lower, fields.at[LO], in_sem.at[1]),
        pltpu.make_async_copy(velocity, fields.at[pl.ds(VZ, 3)], in_sem.at[2]),
        pltpu.make_async_copy(diffusivity, fields.at[DIFF], in_sem.at[3]),
    ]
    for c in loads + field_loads:
        c.start()

    barrier = pltpu.get_barrier_semaphore()

    first_half = (gy & 1) == 0
    mirror = (gx, gy ^ 1, gz)
    sideways = (gx, (gy + jnp.where(first_half, N_Y - 1, 1)) & (N_Y - 1), gz)
    above, below = (gx, gy, (gz + 1) & (N_Z - 1)), (gx, gy, (gz + N_Z - 1) & (N_Z - 1))
    last = gz == N_Z - 1
    bottom = gz == 0
    greets = [(first_half, mirror), (first_half, sideways), (gz < N_Z - 1, above), (bottom, below)]
    answers = [
        (jnp.logical_not(first_half), mirror, 0),
        (jnp.logical_not(first_half), sideways, 1),
        (gz > 0, below, 2),
        (last, above, 3),
    ]

    def tell(when, sem, dev):
        @pl.when(when)
        def _():
            pl.semaphore_signal(sem, inc=1, device_id=dev, device_id_type=MESH)

    same_y = [8 * k for k in range(1, 8)]
    along_y = list(range(1, 8))
    beside = ((gx + jnp.where((gx & 1) == 0, N_X - 1, 1)) & (N_X - 1), gy)
    near_by = [peer(i, gx, gy) for i in same_y + along_y] + [beside]
    for dev in near_by:
        pl.semaphore_signal(barrier, inc=1, device_id=dev + (gz,), device_id_type=MESH)
    for when, dev in greets:
        tell(when, barrier, dev)

    loads[0].wait()
    loads[1].wait()
    blk = blk_v[...]
    block_y = jnp.bitwise_and(blk, 127)
    owner = (blk // 128) * N_Y + block_y // 16
    local = jnp.bitwise_and(block_y, 15).astype(jnp.float32)
    dest = lax.broadcasted_iota(jnp.int32, (OWNERS, 128), 0)
    sensor = lane_of((OWNERS, 128))
    goes = jnp.broadcast_to(owner, (OWNERS, 128)) == dest
    before = jnp.where(dest < sensor, 1.0, 0.0).astype(jnp.bfloat16)
    rank = jnp.dot(
        jnp.where(goes, 1.0, 0.0).astype(jnp.bfloat16), before, preferred_element_type=jnp.float32
    )
    picks = [jnp.logical_and(goes, rank < 0.5), jnp.logical_and(goes, rank > 0.5)]
    meta = jnp.full((OWNERS, 128), -1.0, jnp.float32)
    for r in range(2):
        e = jnp.sum(jnp.where(picks[r], err_v[...], 0.0), axis=1, keepdims=True)
        l = jnp.sum(jnp.where(picks[r], local + 1.0, 0.0), axis=1, keepdims=True) - 1.0
        meta = jnp.where(sensor == 2 * r, e, meta)
        meta = jnp.where(sensor == 2 * r + 1, l, meta)
    swapped = jnp.where((dest & 1) == 0, pltpu.roll(meta, OWNERS - 1, 0), pltpu.roll(meta, 1, 0))
    meta = jnp.where(sensor < 4, meta, pltpu.roll(swapped, 4, 1))
    msg[pl.ds(16, OWNERS, stride=PITCH), :] = meta
    pick = jnp.concatenate([jnp.where(p, 1.0, 0.0) for p in picks], axis=0).astype(jnp.bfloat16)
    loads[2].wait()
    for j in range(8):
        whole = stage[:, j * 128 : (j + 1) * 128]
        part_a = whole.astype(jnp.bfloat16)
        rest = whole - part_a.astype(jnp.float32)
        part_b = rest.astype(jnp.bfloat16)
        part_c = (rest - part_b.astype(jnp.float32)).astype(jnp.bfloat16)
        out = jnp.dot(pick, part_a, preferred_element_type=jnp.float32)
        out += jnp.dot(pick, part_b, preferred_element_type=jnp.float32)
        out += jnp.dot(pick, part_c, preferred_element_type=jnp.float32)
        at = ROW[j // 4] + j % 4
        msg[pl.ds(at, OWNERS, stride=PITCH), :] = out[:OWNERS]
        msg[pl.ds(at + 4, OWNERS, stride=PITCH), :] = out[OWNERS:]

    for c in field_loads:
        c.wait()

    def fill_faces(values, speeds):
        for k, v in enumerate(values):
            zs[0, 8 * k : 8 * k + 8, :] = v[15]
            zs[1, 8 * k : 8 * k + 8, :] = v[0]
            xs[0, 16 * k : 16 * k + 16, :] = v[:, 7, :]
            xs[1, 16 * k : 16 * k + 16, :] = v[:, 0, :]
            t = v.reshape(128, 128).T
            ys[0, k : k + 1, :] = t[127:128]
            ys[1, k : k + 1, :] = t[0:1]
        if speeds is not None:
            vz, vx, vy = speeds
            zs[0, 16:24, :] = vz[15]
            zs[1, 16:24, :] = vz[0]
            xs[0, 32:48, :] = vx[:, 7, :]
            xs[1, 32:48, :] = vx[:, 0, :]
            t = vy.reshape(128, 128).T
            ys[0, 2:3, :] = t[127:128]
            ys[1, 2:3, :] = t[0:1]

    def face_copies(rnd):
        copies = []
        for d in range(2):
            step = 1 if d == 0 else -1
            for k, (src, dst, dev) in enumerate((
                (zs, zr, (gx, gy, lax.rem(gz + step + N_Z, N_Z))),
                (xs, xr, (lax.rem(gx + step + N_X, N_X), gy, gz)),
                (ys, yr, (gx, lax.rem(gy + step + N_Y, N_Y), gz)),
            )):
                n = src.shape[1]
                if rnd == 1 and k < 2:
                    n = n // 3 * 2
                copies.append(
                    pltpu.make_async_remote_copy(
                        src_ref=src.at[d, pl.ds(0, n)],
                        dst_ref=dst.at[rnd, d, pl.ds(0, n)],
                        send_sem=face_send.at[rnd, d, k],
                        recv_sem=face_recv.at[rnd, d, k],
                        device_id=dev,
                        device_id_type=MESH,
                    )
                )
        return copies

    fill_faces([fields[UP], fields[LO]], [fields[VZ], fields[VX], fields[VY]])

    greeted = sum(jnp.where(when, 1, 0) for when, _, _ in answers)
    pl.semaphore_wait(barrier, len(near_by) + greeted)
    for i in along_y:
        pl.semaphore_signal(
            row_sem.at[8 - i], inc=1, device_id=peer(i, gx, gy) + (gz,), device_id_type=MESH
        )
    for when, dev, k in answers:
        tell(when, answer_sem.at[k], dev)

    def slot(px, py, row):
        return pl.multiple_of((px * N_Y + py) * PITCH + row, 8)

    def groups_of(phase):
        return NEAR if phase == 2 else FAR

    def rows_of(phase):
        return WHOLE if phase == 2 else PART[phase]

    def message(i, phase, group):
        px, py = peer(i, gx, gy)
        near = phase // 2
        row, rows = rows_of(phase)
        return pltpu.make_async_remote_copy(
            src_ref=msg.at[pl.ds(slot(px, py if near else py ^ 1, row), rows)],
            dst_ref=got.at[near * HALF + i, pl.ds(row, rows)],
            send_sem=send_sem.at[phase],
            recv_sem=arrive_sem.at[phase, group],
            device_id=(px, py, gz),
            device_id_type=MESH,
        )

    def send_groups(phase, groups):
        for group in groups:
            lo, hi = groups_of(phase)[group]

            def body(i, carry):
                message(i, phase, group).start()
                return carry

            lax.fori_loop(lo, hi, body, 0)

    def send_from(first, step, count):
        def body(k, carry):
            i = first + step * k
            message(i, 0, i >> 4).start()
            return carry

        lax.fori_loop(0, count, body, 0)

    send_from(1, 1, 7)
    send_from(8, 8, 7)
    for dy in (1, 7, 2, 6, 3, 5, 4):
        pl.semaphore_wait(row_sem.at[dy], 1)
        send_from(8 + dy, 8, 7)
    send_groups(1, range(len(FAR)))

    for k, (when, _) in enumerate(greets):

        @pl.when(when)
        def _():
            pl.semaphore_wait(answer_sem.at[k], 1)

    first = face_copies(0)
    for c in first:
        c.start()
    send_groups(2, (0, 1))

    x_of = lax.broadcasted_iota(jnp.int32, (16, 8, 128), 1)
    y_of = lax.broadcasted_iota(jnp.int32, (16, 8, 128), 2)
    inner = [
        (gz > 0, gz < N_Z - 1),
        (gx > 0, gx < N_X - 1),
        (gy > 0, gy < N_Y - 1),
    ]

    def keep(flag, value):
        return jnp.where(flag, value, 0.0)

    def halo(rnd, dim, k, side):
        flag = inner[dim][side]
        if dim == 0:
            return keep(flag, zr[rnd, side, 8 * k : 8 * k + 8, :])[None]
        if dim == 1:
            return keep(flag, xr[rnd, side, 16 * k : 16 * k + 16, :])[:, None, :]
        columns = turned[side][:, k : k + 1]
        return keep(flag, columns).reshape(16, 8, 1)

    def shifted(value, rnd, dim, k):
        below, above = halo(rnd, dim, k, 0), halo(rnd, dim, k, 1)
        if dim == 0:
            return (
                jnp.concatenate([below, value[:15]], axis=0),
                jnp.concatenate([value[1:], above], axis=0),
            )
        if dim == 1:
            return (
                jnp.where(x_of == 0, below, pltpu.roll(value, 1, 1)),
                jnp.where(x_of == 7, above, pltpu.roll(value, 7, 1)),
            )
        return (
            jnp.where(y_of == 0, below, pltpu.roll(value, 1, 2)),
            jnp.where(y_of == 127, above, pltpu.roll(value, 127, 2)),
        )

    turn[...] = jnp.zeros_like(turn)

    def turn_faces(rnd):
        sides = []
        for d in range(2):
            turn[d, 0:8, :] = yr[rnd, d]
            sides.append(turn[d].T)
        return sides

    upper_rows = lax.broadcasted_iota(jnp.int32, (8, 128), 0) < 4
    full = lambda v: jnp.full((8, 128), v, jnp.float32)
    nothing = (full(jnp.inf), full(-jnp.inf))
    pick_of = (jnp.minimum, jnp.maximum)

    def tables(part):
        return tuple(tuple(tabs[part, kind, b] for b in range(16)) for kind in range(2))

    def store(part, t):
        for kind in range(2):
            for b in range(16):
                tabs[part, kind, b] = t[kind][b]

    def spread(m, row, near):
        for k in range(2):
            a, b = (
                jnp.broadcast_to(row[:, lane : lane + 1], (8, 128))
                for lane in (4 * near + k, 4 * near + k + 2)
            )
            wide[2 * m + k] = jnp.where(upper_rows, a, b)

    def begin(near):
        py = gy if near else gy ^ 1
        spread(0, msg[pl.ds(slot(gx, gy ^ 1, 16), 8), :][0:1], near)
        start = tuple((nothing[kind],) * 16 for kind in range(2))
        for part in range(2):
            store(part, merge(start, msg[pl.ds(slot(gx, py, ROW[part]), 8), :], wide[0], wide[1]))

    def arrived(phase, group):
        lo, hi = groups_of(phase)[group]
        row, rows = rows_of(phase)
        block_of = got.at[pl.ds(phase // 2 * HALF + lo, hi - lo), pl.ds(row, rows)]
        return pltpu.make_async_remote_copy(
            src_ref=block_of,
            dst_ref=block_of,
            send_sem=send_sem.at[phase],
            recv_sem=arrive_sem.at[phase, group],
            device_id=mirror,
            device_id_type=MESH,
        )

    def await_group(phase, group):
        near = phase // 2
        lo, hi = groups_of(phase)[group]
        n = hi - lo
        arrived(phase, group).wait_recv()
        for m in range(n):
            spread(m, got[lo + m, 16:17, :], near)
        for part in (0, 1) if near else (phase,):

            def one(m, t):
                rows = got[near * HALF + lo + m, ROW[part] : ROW[part] + 8, :]
                return merge(t, rows, wide[2 * m], wide[2 * m + 1])

            def body(h, t):
                return one(2 * h + 1, one(2 * h, t))

            t = lax.fori_loop(0, n // 2, body, tables(part))
            store(part, one(n - 1, t) if n % 2 else t)

    def folded(part, kind, b):
        t = tabs[part, kind, b]
        return pick_of[kind](t, pltpu.roll(t, 4, 0))

    def hand_over(part):
        return pltpu.make_async_remote_copy(
            src_ref=relay.at[part],
            dst_ref=relayed.at[part],
            send_sem=relay_sem.at[0, part],
            recv_sem=relay_sem.at[1, part],
            device_id=mirror,
            device_id_type=MESH,
        )

    def far_part(part):
        for group in range(len(FAR)):
            await_group(part, group)
        for kind in range(2):
            for b in range(8):
                relay[part, kind, b] = jnp.where(
                    upper_rows, folded(part, kind, b), folded(part, kind, b + 8)
                )
        hand_over(part).start()

    begin(0)
    far_part(0)

    for c in first:
        c.wait()
    turned = turn_faces(0)
    diff = fields[DIFF]
    centre = 1.0 - 6.0 * diff
    for dim, which in enumerate((VZ, VX, VY)):
        v = fields[which]
        centre = centre - jnp.abs(v)
        v_below, v_above = shifted(v, 0, dim, 2)
        coefs[2 * dim] = jnp.maximum(v_below, 0.0) + diff
        coefs[2 * dim + 1] = jnp.maximum(-v_above, 0.0) + diff
    coefs[6] = centre

    def advance(rnd):
        results = []
        for k in range(2):
            value = fields[k]
            total = coefs[6] * value
            for dim in range(3):
                below, above = shifted(value, rnd, dim, k)
                total = total + coefs[2 * dim] * below + coefs[2 * dim + 1] * above
            results.append(total)
        return results

    once = advance(0)
    fields[UP] = once[0]
    fields[LO] = once[1]
    fill_faces([fields[UP], fields[LO]], None)
    second = face_copies(1)
    for c in second:
        c.start()
    send_groups(2, (2, 3, 4))

    far_part(1)

    begin(1)
    for group in range(STEP_AFTER):
        await_group(2, group)

    for c in second:
        c.wait()
    turned = turn_faces(1)
    twice = advance(1)
    fields[UP] = twice[0]
    fields[LO] = twice[1]

    for group in range(STEP_AFTER, len(NEAR) - 1):
        await_group(2, group)
    for part in range(2):
        hand_over(part).wait_recv()
        for kind in range(2):
            for b in range(8):
                came = relayed[part, kind, b]
                for block_at, where in ((b, upper_rows), (b + 8, jnp.logical_not(upper_rows))):
                    tabs[part, kind, block_at] = pick_of[kind](
                        tabs[part, kind, block_at], jnp.where(where, came, nothing[kind])
                    )
    await_group(2, len(NEAR) - 1)

    for kind, (which, out) in enumerate(((UP, both_out.at[0]), (LO, both_out.at[1]))):
        rows = regroup(
            [jnp.where(upper_rows, folded(0, kind, b), folded(1, kind, b)) for b in range(16)]
        )
        for g in range(16):
            flat[pl.ds(g, 8, stride=16), :] = rows[g]
        out[...] = pick_of[kind](fields[which], flat[...].reshape(16, 8, 128))

    for phase in range(3):
        for group in range(len(groups_of(phase))):
            arrived(phase, group).wait_send()
    for part in range(2):
        hand_over(part).wait_send()


def shards(*args):
    f32 = jnp.float32
    dma = pltpu.SemaphoreType.DMA
    both = pl.pallas_call(
        kernel,
        out_shape=pltpu.VMEM((2, 16, 8, 128), f32),
        in_specs=[pl.BlockSpec(memory_space=pl.ANY)] * 7,
        out_specs=pl.BlockSpec(memory_space=pltpu.VMEM),
        scratch_shapes=[
            pltpu.VMEM((6, 16, 8, 128), f32),
            pltpu.VMEM((7, 16, 8, 128), f32),
            pltpu.VMEM((128, 1024), f32),
            pltpu.VMEM((1, 128), f32),
            pltpu.VMEM((1, 128), jnp.int32),
            pltpu.VMEM((OWNERS * PITCH, 128), f32),
            pltpu.VMEM((OWNERS, PITCH, 128), f32),
            pltpu.VMEM((2, 2, 16, 8, 128), f32),
            pltpu.VMEM((128, 128), f32),
            pltpu.VMEM((2, 24, 128), f32),
            pltpu.VMEM((2, 2, 24, 128), f32),
            pltpu.VMEM((2, 48, 128), f32),
            pltpu.VMEM((2, 2, 48, 128), f32),
            pltpu.VMEM((2, 8, 128), f32),
            pltpu.VMEM((2, 2, 8, 128), f32),
            pltpu.VMEM((2, 128, 128), f32),
            pltpu.VMEM((64, 8, 128), f32),
            pltpu.VMEM((2, 2, 8, 8, 128), f32),
            pltpu.VMEM((2, 2, 8, 8, 128), f32),
            dma((4,)),
            dma((3,)),
            dma((3,)),
            dma((3, len(NEAR))),
            dma((2, 2)),
            dma((2, 2, 3)),
            dma((2, 2, 3)),
            pltpu.SemaphoreType.REGULAR((4,)),
            pltpu.SemaphoreType.REGULAR((8,)),
        ],
        compiler_params=pltpu.CompilerParams(
            collective_id=0, has_side_effects=True, vmem_limit_bytes=32 << 20
        ),
        cost_estimate=pl.CostEstimate(flops=10**8, bytes_accessed=2 << 20, transcendentals=0),
    )(*[pltpu.with_memory_space_constraint(a, pltpu.HBM) for a in args])
    return both[0], both[1]


def solution(mesh):
    in_specs = (
        P("gz", "gx", "gy"),
        P("gz", "gx", "gy"),
        P(None, "gz", "gx", "gy"),
        P("gz", "gx", "gy"),
        P("gz", ("gx", "gy"), None),
        P("gz", ("gx", "gy")),
        P("gz", ("gx", "gy")),
    )
    out_specs = (P("gz", "gx", "gy"), P("gz", "gx", "gy"))
    return jax.shard_map(shards, mesh=mesh, in_specs=in_specs, out_specs=out_specs, check_vma=False)
```
